128 devices in a mesh: dp: 8 (over x_hi, z), mp: 16 (over x_lo, y, core).
Axes of the slice: x: 4 (x_hi: 2, x_lo: 2; x = x_hi * 2 + x_lo), y: 4, z: 4, core: 2. Of those that a mesh axis runs over, the one named last changes fastest.
Arguments:
- tokens: bfloat16 [4096, 6144], P('dp'), may hold values from -6 to 6, as said below
- norm_gain: float32 [6144], replicated, may hold values from 0.5 to 1.5
- qkv_weight: bfloat16 [6144, 3, 4096], P('dp', None, 'mp'), as said below
- qk_gains: float32 [2, 128], replicated, may hold values from 0.6 to 6, as said below
- in_weight: bfloat16 [6144, 12288], P('dp', 'mp'), may hold values from -0.078125 to 0.078125
- in_bias: float32 [12288], P('mp'), may hold values from -3 to 3
- out_weight: bfloat16 [4096, 6144], P('mp', 'dp'), may hold values from -0.09375 to 0.09375
- mlp_out_weight: bfloat16 [12288, 6144], P('mp', 'dp'), may hold values from -0.0546875 to 0.0546875
- out_bias: float32 [6144], replicated, may hold values from -3 to 3
- targets: bfloat16 [4096, 3072], P('dp'), may hold values from -6 to 6
Outputs:
- gram_matrix: float32 [6144, 6144], P('mp', 'dp')
- cross_matrix: float32 [6144, 3072], P('mp', 'dp')
The draws below stay inside these ranges and needn't reach their ends.
Inputs may be any that keep to these rules, and one draw needn't show every extreme that they name: `tokens`: activations of order one. `qkv_weight`: entries of order one over the square root of 6144. `qk_gains`: positive gains.
All inputs are finite; a program needn't handle non-finite values.
Results may differ from the reference program's by a relative error of at most 0.025.
Values may be sent and summed in bfloat16 or wider, within the bound.
No kernel may reach another device: no remote copies, remote signals or barrier semaphores. Data moves between devices by JAX's collectives and lax.ppermute only.
A program may use at most 128 MiB of HBM per device.

```python
import jax
import jax.numpy as jnp
from jax import lax

D = 6144
HEADS = 32
HEAD = 128
FF = 12288
ZW = 3072
TOK_DEV = 512
TOKENS = 4096
N_DP = 8
N_MP = 16


def draw_tokens(key, part):
    key = jax.random.fold_in(key, 5)
    base_key = jax.random.fold_in(key, 0)
    values = jax.random.normal(base_key, (TOKENS, D), jnp.float32)
    return jnp.clip(values, -6.0, 6.0).astype(jnp.bfloat16)


def draw_qkv_weight(key, part):
    key = jax.random.fold_in(key, 11)
    weight_key = jax.random.fold_in(key, 0)
    limit = (3.0 / D) ** 0.5
    weights = jax.random.uniform(weight_key, (D, 3, HEADS * HEAD), jnp.float32, -limit, limit)
    return weights.astype(jnp.bfloat16)


def draw_qk_gains(key, part):
    key = jax.random.fold_in(key, 23)
    return jax.random.uniform(key, (2, HEAD), jnp.float32, 0.6, 1.4)


def shard_levels(stream_key, shape, cuts, smallest, largest):
    gain, own = 1.0, jax.random.fold_in(stream_key, 6)
    for axis_at, shards_of in cuts:
        draws = jnp.exp(jax.random.uniform(jax.random.fold_in(own, axis_at), (shards_of,), jnp.float32, smallest / len(cuts), largest / len(cuts)))
        gain = gain * jnp.repeat(draws, shape[axis_at] // shards_of).reshape([-1 if axis == axis_at else 1 for axis in range(len(shape))])
    return gain


def bell_draw(own_key, dims, deviation, bound, cuts=(), dtype=jnp.bfloat16):
    array = jax.random.normal(own_key, dims, jnp.float32) * deviation
    if len(cuts) > 0:
        array = shard_levels(own_key, dims, cuts, -0.22, 0.18) * array
    return jnp.clip(array, min=-bound, max=bound).astype(dtype)


def setup_inputs(seed: int = 0) -> dict:
    key_list = jax.random.split(jax.random.key(seed), 11)
    tokens = draw_tokens(jax.random.fold_in(key_list[10], 71), 0)
    norm_gain = jnp.clip(1.0 + 0.1 * jax.random.normal(key_list[1], (D,), jnp.float32), 0.5, 1.5)
    qkv_weight = draw_qkv_weight(jax.random.fold_in(key_list[10], 71), 0)
    qk_gains = draw_qk_gains(jax.random.fold_in(key_list[10], 71), 0)
    in_weight = bell_draw(key_list[4], (D, FF), D ** -0.5, 0.078125, ((0, 8), (1, 16)))
    in_bias = bell_draw(key_list[5], (FF,), 0.5, 3.0, ((0, 16),), jnp.float32)
    out_weight = bell_draw(key_list[6], (HEADS * HEAD, D), (HEADS * HEAD) ** -0.5, 0.09375, ((0, 16), (1, 8)))
    mlp_out_weight = bell_draw(key_list[7], (FF, D), FF ** -0.5, 0.0546875, ((0, 16), (1, 8)))
    out_bias = bell_draw(key_list[8], (D,), 0.5, 3.0, (), jnp.float32)
    targets = bell_draw(key_list[9], (TOKENS, ZW), 1.0, 6.0, ((0, 8),))
    return {"tokens": tokens, "norm_gain": norm_gain, "qkv_weight": qkv_weight, "qk_gains": qk_gains, "in_weight": in_weight, "in_bias": in_bias, "out_weight": out_weight, "mlp_out_weight": mlp_out_weight, "out_bias": out_bias, "targets": targets}


def layer_norm(inputs, norm_scale):
    center = lax.optimization_barrier(jnp.mean(inputs, axis=-1, keepdims=True))
    spread = lax.optimization_barrier(jnp.mean(jnp.square(inputs - center), axis=-1, keepdims=True))
    return (inputs - center) * lax.rsqrt(spread + 1e-06) * norm_scale

def reference(tokens, norm_gain, qkv_weight, qk_gains, in_weight, in_bias, out_weight, mlp_out_weight, out_bias, targets):
    token_values = tokens.astype(jnp.float32)
    normed = layer_norm(token_values, norm_gain).astype(jnp.bfloat16)
    projected = jnp.dot(normed, qkv_weight.reshape(D, 3 * HEADS * HEAD), preferred_element_type=jnp.float32)
    projected = projected.reshape(TOKENS, 3, HEADS, HEAD)
    queries = layer_norm(projected[:, 0], qk_gains[0]).astype(jnp.bfloat16).transpose(1, 0, 2)
    all_keys = layer_norm(projected[:, 1], qk_gains[1]).astype(jnp.bfloat16).transpose(1, 0, 2)
    values = projected[:, 2].astype(jnp.bfloat16).transpose(1, 0, 2)

    def one_head(operands):
        head_queries, head_keys, head_values = operands
        scores = jnp.dot(head_queries, head_keys.T, preferred_element_type=jnp.float32) * HEAD ** (-0.5)
        soft_weights = jax.nn.softmax(scores, axis=-1).astype(jnp.bfloat16)
        return jnp.dot(soft_weights, head_values, preferred_element_type=jnp.float32).astype(jnp.bfloat16)
    attended = lax.map(one_head, (queries, all_keys, values))
    attended = attended.transpose(1, 0, 2).reshape(TOKENS, HEADS * HEAD)
    mlp_input = jnp.dot(normed, in_weight, preferred_element_type=jnp.float32) + in_bias
    hidden = jax.nn.gelu(mlp_input, approximate=False).astype(jnp.bfloat16)
    attn_blocks = attended.reshape(TOKENS, N_MP, HEADS * HEAD // N_MP).transpose(1, 0, 2)
    hidden_blocks = hidden.reshape(TOKENS, N_MP, FF // N_MP).transpose(1, 0, 2)
    out_blocks = out_weight.reshape(N_MP, HEADS * HEAD // N_MP, D)
    mlp_blocks = mlp_out_weight.reshape(N_MP, FF // N_MP, D)

    def add_block(running, pieces):
        attn_piece, hidden_piece, out_piece, mlp_piece = pieces
        partial_sum = jnp.dot(attn_piece, out_piece, preferred_element_type=jnp.float32)
        partial_sum = partial_sum + jnp.dot(hidden_piece, mlp_piece, preferred_element_type=jnp.float32)
        rounded = lax.optimization_barrier(partial_sum.astype(jnp.bfloat16))
        return (running + rounded.astype(jnp.float32), None)
    summed, _ = lax.scan(add_block, jnp.zeros((TOKENS, D), jnp.float32), (attn_blocks, hidden_blocks, out_blocks, mlp_blocks))
    block_output = (token_values + out_bias + summed).astype(jnp.bfloat16)
    output_blocks = block_output.reshape(N_DP, TOK_DEV, D)
    target_blocks = targets.reshape(N_DP, TOK_DEV, ZW)

    def add_moments(running, pieces):
        output_piece, target_piece = pieces
        gram_part = jnp.einsum('ti,tj->ij', output_piece, output_piece, preferred_element_type=jnp.float32) / TOKENS
        cross_part = jnp.einsum('ti,tj->ij', output_piece, target_piece, preferred_element_type=jnp.float32) / TOKENS
        gram_part = lax.optimization_barrier(gram_part.astype(jnp.bfloat16)).astype(jnp.float32)
        cross_part = lax.optimization_barrier(cross_part.astype(jnp.bfloat16)).astype(jnp.float32)
        return ((running[0] + gram_part, running[1] + cross_part), None)
    start_value = (jnp.zeros((D, D), jnp.float32), jnp.zeros((D, ZW), jnp.float32))
    (gram_matrix, cross_matrix), _ = lax.scan(add_moments, start_value, (output_blocks, target_blocks))
    return (gram_matrix, cross_matrix)
```

```python
import jax
import jax.numpy as jnp
from jax import lax
from jax.sharding import Mesh, PartitionSpec as P

HEAD = 128
BF = jnp.bfloat16
F32 = jnp.float32


def layer_norm(inputs, norm_scale):
    center = jnp.mean(inputs, axis=-1, keepdims=True)
    spread = jnp.mean(jnp.square(inputs - center), axis=-1, keepdims=True)
    return (inputs - center) * lax.rsqrt(spread + 1e-06) * norm_scale


def swap(x, axis, mask):
    size = lax.axis_size(axis)
    return lax.ppermute(x, axis, [(i, i ^ mask) for i in range(size)])


def shift(x, axis, step):
    size = lax.axis_size(axis)
    return lax.ppermute(x, axis, [(i, (i + step) % size) for i in range(size)])


def dyn(x, start, size, axis):
    return lax.dynamic_slice_in_dim(x, start, size, axis)


def dot(a, b):
    return jnp.dot(a, b, preferred_element_type=F32)


def ring_gather(x, axis):
    below = shift(x, axis, 1)
    above = shift(x, axis, -1)
    half = x.shape[0] // 2
    far = jnp.concatenate([shift(below[:half], axis, 1), shift(above[half:], axis, -1)])
    return [x, below, far, above]


def place(blocks, index, count, rows):
    out = jnp.zeros((count * rows,) + blocks[0].shape[1:], blocks[0].dtype)
    for distance, block in enumerate(blocks):
        at = lax.rem(index - distance + count, count)
        out = lax.dynamic_update_slice_in_dim(out, block, at * rows, 0)
    return out


def on_device(
    tokens,
    norm_gain,
    qkv_weight,
    qk_gains,
    in_weight,
    in_bias,
    out_weight,
    mlp_out_weight,
    out_bias,
    targets,
):
    xh, z, xl, y, c = (lax.axis_index(a) for a in ("xh", "z", "xl", "y", "c"))
    rows, width = tokens.shape
    half = width // 2
    block = width // 8
    target_block = targets.shape[1] // 8
    piece = rows // 16

    by_head = qkv_weight.reshape(block, 3, 2, HEAD)
    keep_qkv = dyn(by_head, xh, 1, 2).reshape(block, 3 * HEAD)
    give_qkv = dyn(by_head, 1 - xh, 1, 2).reshape(block, 3 * HEAD)
    hid = in_weight.shape[1] // 2
    keep_in = dyn(in_weight, xh * hid, hid, 1)
    give_in = dyn(in_weight, (1 - xh) * hid, hid, 1)
    got_qkv = swap(give_qkv, "xh", 1)
    qkv_own = lax.all_gather(keep_qkv, "z", axis=0, tiled=True)
    qkv_par = lax.all_gather(got_qkv, "z", axis=0, tiled=True)

    token_values = tokens.astype(F32)
    center = jnp.mean(token_values, axis=-1, keepdims=True)
    spread = jnp.mean(jnp.square(token_values - center), axis=-1, keepdims=True)
    scale = lax.rsqrt(spread + 1e-06)

    def normed_half(which):
        part = dyn(tokens, which * half, half, 1).astype(F32)
        gain = dyn(norm_gain, which * half, half, 0)
        return ((part - center) * scale * gain).astype(BF)

    norm_own, norm_par = normed_half(xh), normed_half(1 - xh)
    share = rows // 8

    def from_partner(x):
        mine = dyn(x, (y * 2 + c) * share, share, 0)
        got = swap(mine, "xh", 1)
        around = place(ring_gather(got, "y"), y, 4, share)
        other = swap(around, "c", 1)
        first = jnp.where(c == 0, around, other).reshape(4, 1, share, half)
        second = jnp.where(c == 0, other, around).reshape(4, 1, share, half)
        return jnp.concatenate([first, second], axis=1).reshape(rows, half)

    far_own, far_par = from_partner(norm_par), from_partner(norm_own)
    got_in = swap(give_in, "xh", 1)
    in_own = lax.all_gather(keep_in, "z", axis=0, tiled=True)
    in_par = lax.all_gather(got_in, "z", axis=0, tiled=True)

    left = jnp.concatenate([norm_own, far_own])
    right = jnp.concatenate([norm_par, far_par])
    qkv = dot(left, qkv_own) + dot(right, qkv_par)
    queries = layer_norm(qkv[:, :HEAD], qk_gains[0]).astype(BF)
    own_keys = layer_norm(qkv[:, HEAD : 2 * HEAD], qk_gains[1]).astype(BF)
    own_kv = jnp.concatenate([own_keys, qkv[:, 2 * HEAD :].astype(BF)], axis=1)
    all_kv = lax.all_gather(own_kv, "z", axis=0, tiled=True)

    bias = dyn(in_bias, xh * hid, hid, 0)
    mlp_input = dot(left, in_own) + dot(right, in_par)
    hidden = jax.nn.gelu(mlp_input + bias, approximate=False).astype(BF)

    far_out, far_mlp = swap(out_weight, "xh", 1), swap(mlp_out_weight, "xh", 1)

    def to_tokens(x):
        got = swap(x[rows:], "xh", 1)
        mine = x[:rows]
        mine = jnp.where(xh == 0, jnp.concatenate([mine, got], axis=1), jnp.concatenate([got, mine], axis=1))
        return lax.all_gather(mine, "z", axis=0, tiled=False)

    hidden = to_tokens(hidden)

    all_keys, all_values = all_kv[:, :HEAD], all_kv[:, HEAD:]
    scores = jnp.einsum("qd,kd->qk", queries, all_keys, preferred_element_type=F32) * HEAD ** (-0.5)
    soft_weights = jax.nn.softmax(scores, axis=-1).astype(BF)
    attended = dot(soft_weights, all_values).astype(BF)
    attended = to_tokens(attended)

    at = ((c * 4 + y) * 2 + xl) * piece
    own_rows = dyn(tokens, at, piece, 0).reshape(piece, 2, 4, block).transpose(2, 0, 1, 3)
    residual = lax.all_to_all(own_rows, "z", split_axis=0, concat_axis=0, tiled=True)
    own_targets = dyn(targets, at, piece, 0).reshape(piece, 8, target_block).transpose(1, 0, 2)
    own_targets = lax.all_to_all(own_targets, ("xh", "z"), split_axis=0, concat_axis=0, tiled=True)
    all_targets = lax.all_gather(own_targets, ("xl", "y", "c"), axis=0, tiled=True)

    part_rows = rows // 2

    def partial(start, out_w, mlp_w):
        a = dyn(attended, start, part_rows, 1).reshape(4 * part_rows, -1)
        h = dyn(hidden, start, part_rows, 1).reshape(4 * part_rows, -1)
        return (dot(a, out_w) + dot(h, mlp_w)).reshape(4, part_rows, block)

    def over_core(out_w, mlp_w):
        give = partial((1 - c) * part_rows, out_w, mlp_w).astype(BF)
        got = swap(give, "c", 1)
        return partial(c * part_rows, out_w, mlp_w) + got.astype(F32)

    quarter = part_rows // 4

    def over_y(x, first, second):
        def at_index(i):
            return dyn(x, i * quarter, quarter, 1)

        third = first ^ second
        one = swap(at_index(y ^ third).astype(BF), "y", first)
        two = swap(at_index(y ^ first).astype(BF), "y", first)
        far = at_index(y ^ second) + one.astype(F32)
        return at_index(y) + two.astype(F32) + swap(far.astype(BF), "y", second).astype(F32)

    def over_xl(x):
        got = swap(dyn(x, (1 - xl) * piece, piece, 1).astype(BF), "xl", 1)
        return dyn(x, xl * piece, piece, 1) + got.astype(F32)

    sum_own = over_xl(over_y(over_core(out_weight, mlp_out_weight), 1, 3))
    sum_par = over_xl(over_y(over_core(far_out, far_mlp), 3, 1))

    def finish(total, which):
        base = dyn(residual, which, 1, 2).reshape(4, piece, block).astype(F32)
        return (base + dyn(out_bias, (which * 4 + z) * block, block, 0) + total).astype(BF)

    mine = finish(sum_own, xh)
    theirs = swap(finish(sum_par, 1 - xh), "xh", 1)
    out_piece = jnp.where(xh == 0, jnp.concatenate([mine, theirs]), jnp.concatenate([theirs, mine]))
    out_piece = out_piece.reshape(8 * piece, block)

    columns = lax.all_gather(out_piece, ("xl", "y", "c"), axis=0, tiled=True)
    turned = lax.ppermute(
        out_piece,
        ("xh", "z", "xl", "y"),
        [(a * 8 + b, b * 8 + a) for a in range(8) for b in range(8)],
    )
    narrow = block // 2
    stay = dyn(turned, c * narrow, narrow, 1)
    come = swap(dyn(turned, (1 - c) * narrow, narrow, 1), "c", 1)
    pair = jnp.where(c == 0, jnp.concatenate([stay, come]), jnp.concatenate([come, stay]))
    own_columns = lax.all_gather(pair, ("xh", "z"), axis=0, tiled=True)

    total_tokens = rows * 8
    gram = jnp.einsum("ti,tj->ij", own_columns, columns, preferred_element_type=F32) / total_tokens
    all_targets = all_targets.reshape(total_tokens, target_block)
    cross = jnp.einsum("ti,tj->ij", own_columns, all_targets, preferred_element_type=F32) / total_tokens
    return gram, cross


def solution(mesh):
    fine = Mesh(mesh.devices.reshape(2, 4, 2, 4, 2), ("xh", "z", "xl", "y", "c"))
    dp, mp = ("xh", "z"), ("xl", "y", "c")
    placed = (
        P(dp, None),
        P(),
        P(dp, None, mp),
        P(),
        P(dp, mp),
        P(mp),
        P(mp, dp),
        P(mp, dp),
        P(),
        P(dp, None),
    )
    return jax.shard_map(
        on_device,
        mesh=fine,
        in_specs=placed,
        out_specs=(P(mp, dp), P(mp, dp)),
        check_vma=False,
    )
```

```python
import jax
import jax.numpy as jnp
from jax import lax
from jax.sharding import Mesh, PartitionSpec as P

HEAD = 128
BF = jnp.bfloat16
F32 = jnp.float32


def layer_norm(inputs, norm_scale):
    center = jnp.mean(inputs, axis=-1, keepdims=True)
    spread = jnp.mean(jnp.square(inputs - center), axis=-1, keepdims=True)
    return (inputs - center) * lax.rsqrt(spread + 1e-06) * norm_scale


def swap(x, axis, mask):
    size = lax.axis_size(axis)
    return lax.ppermute(x, axis, [(i, i ^ mask) for i in range(size)])


def shift(x, axis, step):
    size = lax.axis_size(axis)
    return lax.ppermute(x, axis, [(i, (i + step) % size) for i in range(size)])


def dyn(x, start, size, axis):
    return lax.dynamic_slice_in_dim(x, start, size, axis)


def dot(a, b):
    return jnp.dot(a, b, preferred_element_type=F32)


def ring_gather(x, axis):
    below = shift(x, axis, 1)
    above = shift(x, axis, -1)
    half = x.shape[0] // 2
    far_low = shift(below[:half], axis, 1)
    far_high = shift(above[half:], axis, -1)
    return [x, above, jnp.concatenate([far_low, far_high]), below]


def in_order(blocks, index):
    count = len(blocks)
    laid = [lax.select_n(lax.rem(i - index + count, count), *blocks) for i in range(count)]
    return jnp.concatenate(laid)


def both(flag, first, second, axis=0):
    return jnp.where(
        flag == 0,
        jnp.concatenate([first, second], axis=axis),
        jnp.concatenate([second, first], axis=axis),
    )


def on_device(
    tokens,
    norm_gain,
    qkv_weight,
    qk_gains,
    in_weight,
    in_bias,
    out_weight,
    mlp_out_weight,
    out_bias,
    targets,
):
    xh, z, xl, y, c = (lax.axis_index(a) for a in ("xh", "z", "xl", "y", "c"))
    rows, width = tokens.shape
    half = width // 2
    block = width // 8
    target_block = targets.shape[1] // 8
    piece = rows // 16

    qkv_rows = lax.all_gather(qkv_weight.reshape(block, 6 * HEAD), "z", axis=0, tiled=True)
    in_rows = lax.all_gather(in_weight, "z", axis=0, tiled=True)

    at = ((c * 4 + y) * 2 + xl) * piece
    base_rows = dyn(tokens, at, piece, 0).reshape(piece, 8, block)
    goal_rows = dyn(targets, at, piece, 0).reshape(piece, 8, target_block)
    spread_rows = jnp.concatenate([base_rows, goal_rows], axis=2).transpose(1, 0, 2)
    own_spread = lax.all_to_all(spread_rows, ("xh", "z"), split_axis=0, concat_axis=0, tiled=True)

    token_values = tokens.astype(F32)
    center = jnp.mean(token_values, axis=-1, keepdims=True)
    spread = jnp.mean(jnp.square(token_values - center), axis=-1, keepdims=True)
    scale = lax.rsqrt(spread + 1e-06)

    def normed_part(start, count, which):
        part = dyn(dyn(tokens, start, count, 0), which * half, half, 1).astype(F32)
        gain = dyn(norm_gain, which * half, half, 0)
        shift_rows, scale_rows = dyn(center, start, count, 0), dyn(scale, start, count, 0)
        return ((part - shift_rows) * scale_rows * gain).astype(BF)

    share = rows // 8
    got = swap(normed_part((c * 4 + y) * share, share, 1 - xh), "xh", 1)
    norm_own = normed_part(0, rows, xh)
    got, out_weight, mlp_out_weight = lax.optimization_barrier((got, out_weight, mlp_out_weight))
    around = in_order(ring_gather(got, "y"), y)
    norm_far = both(c, around, swap(around, "c", 1))

    far_out, far_mlp = swap(out_weight, "xh", 1), swap(mlp_out_weight, "xh", 1)

    qkv_own = dot(norm_own, qkv_rows).reshape(rows, 3, 2, HEAD)
    qkv_far = dot(norm_far, qkv_rows).reshape(rows, 3, 2, HEAD)

    def head_of(x, which):
        return dyn(x, which, 1, 2).reshape(rows, 3 * HEAD)

    give = jnp.concatenate([head_of(qkv_far, 1 - xh), head_of(qkv_own, 1 - xh)]).astype(BF)
    keep = jnp.concatenate([head_of(qkv_own, xh), head_of(qkv_far, xh)])
    qkv = keep + swap(give, "xh", 1).astype(F32)
    queries = layer_norm(qkv[:, :HEAD], qk_gains[0]).astype(BF)
    own_keys = layer_norm(qkv[:, HEAD : 2 * HEAD], qk_gains[1]).astype(BF)
    own_kv = jnp.concatenate([own_keys, qkv[:, 2 * HEAD :].astype(BF)], axis=1)
    all_kv = jnp.concatenate(ring_gather(own_kv, "z"))

    mlp_far = swap(dot(norm_far, in_rows).astype(BF), "xh", 1)
    mlp_input = dot(norm_own, in_rows) + mlp_far.astype(F32)
    hidden = jax.nn.gelu(mlp_input + in_bias, approximate=False).astype(BF)
    hidden = jnp.stack(ring_gather(hidden, "z"))

    all_keys, all_values = all_kv[:, :HEAD], all_kv[:, HEAD:]
    scores = jnp.einsum("qd,kd->qk", queries, all_keys, preferred_element_type=F32) * HEAD ** (-0.5)
    soft_weights = jax.nn.softmax(scores, axis=-1).astype(BF)
    attended = dot(soft_weights, all_values).astype(BF)
    attended = both(xh, attended[:rows], swap(attended[rows:], "xh", 1), axis=1)
    attended = jnp.stack(ring_gather(attended, "z"))

    part_rows = rows // 2

    def partial(start, out_w, mlp_w):
        a = dyn(attended, start, part_rows, 1).reshape(4 * part_rows, -1)
        h = dyn(hidden, start, part_rows, 1).reshape(4 * part_rows, -1)
        return (dot(a, out_w) + dot(h, mlp_w)).reshape(4, part_rows, block)

    def over_core(out_w, mlp_w):
        give = partial((1 - c) * part_rows, out_w, mlp_w).astype(BF)
        got = swap(give, "c", 1)
        return partial(c * part_rows, out_w, mlp_w) + got.astype(F32)

    quarter = part_rows // 4

    def over_y(x, first, second):
        def at_index(i):
            return dyn(x, i * quarter, quarter, 1)

        third = first ^ second
        one = swap(at_index(y ^ third).astype(BF), "y", first)
        two = swap(at_index(y ^ first).astype(BF), "y", first)
        far = at_index(y ^ second) + one.astype(F32)
        return at_index(y) + two.astype(F32) + swap(far.astype(BF), "y", second).astype(F32)

    def over_xl(x):
        got = swap(dyn(x, (1 - xl) * piece, piece, 1).astype(BF), "xl", 1)
        return dyn(x, xl * piece, piece, 1) + got.astype(F32)

    sum_par = over_xl(over_y(over_core(far_out, far_mlp), 3, 1))
    sum_own = over_xl(over_y(over_core(out_weight, mlp_out_weight), 1, 3))
    theirs = swap(sum_par.astype(BF), "xh", 1).astype(F32)
    total = both(xh, in_order([sum_own[i] for i in range(4)], z), in_order([theirs[i] for i in range(4)], z))
    base = own_spread[:, :, :block].reshape(8 * piece, block).astype(F32)
    bias = dyn(out_bias, (xh * 4 + z) * block, block, 0)
    out_piece = (base + bias + total).astype(BF)

    turned = lax.ppermute(
        out_piece,
        ("xh", "z", "xl", "y"),
        [(a * 8 + b, b * 8 + a) for a in range(8) for b in range(8)],
    )
    narrow = block // 2
    stay = dyn(turned, c * narrow, narrow, 1)
    come = swap(dyn(turned, (1 - c) * narrow, narrow, 1), "c", 1)
    own_columns = lax.all_gather(both(c, stay, come), ("xh", "z"), axis=0, tiled=True)

    total_tokens = rows * 8
    over_xl_pair = both(xl, out_piece, swap(out_piece, "xl", 1))
    by_place = own_columns.reshape(2, 4, 16 * piece, narrow)
    gram = 0.0
    for distance, part in enumerate(ring_gather(over_xl_pair, "y")):
        other = swap(part, "c", 1)
        part, other = part.reshape(2, 8 * piece, block), other.reshape(2, 8 * piece, block)
        mine = dyn(by_place, lax.rem(y + distance, 4), 1, 1).reshape(2, 16 * piece, narrow)
        full = both(c, part, other, axis=1)
        gram = gram + jnp.einsum("ati,atj->ij", mine, full, preferred_element_type=F32)
    all_targets = lax.all_gather(own_spread[:, :, block:], ("xl", "y", "c"), axis=0, tiled=True)
    all_targets = all_targets.reshape(total_tokens, target_block)
    cross = jnp.einsum("ti,tj->ij", own_columns, all_targets, preferred_element_type=F32)
    return gram / total_tokens, cross / total_tokens


def solution(mesh):
    fine = Mesh(mesh.devices.reshape(2, 4, 2, 4, 2), ("xh", "z", "xl", "y", "c"))
    dp, mp = ("xh", "z"), ("xl", "y", "c")
    placed = (
        P(dp, None),
        P(),
        P(dp, None, mp),
        P(),
        P(dp, mp),
        P(mp),
        P(mp, dp),
        P(mp, dp),
        P(),
        P(dp, None),
    )
    return jax.shard_map(
        on_device,
        mesh=fine,
        in_specs=placed,
        out_specs=(P(mp, dp), P(mp, dp)),
        check_vma=False,
    )
```

```python
import functools

import jax
import jax.numpy as jnp
from jax import lax
from jax.experimental import pallas as pl
from jax.experimental.pallas import tpu as pltpu
from jax.sharding import Mesh, PartitionSpec as P

HEAD = 128
BF = jnp.bfloat16
F32 = jnp.float32
LOG2E = 1.4426950408889634


def layer_norm(inputs, norm_scale):
    center = jnp.mean(inputs, axis=-1, keepdims=True)
    spread = jnp.mean(jnp.square(inputs - center), axis=-1, keepdims=True)
    return (inputs - center) * lax.rsqrt(spread + 1e-06) * norm_scale


def swap(x, axis, mask=1):
    size = lax.axis_size(axis)
    return lax.ppermute(x, axis, [(i, i ^ mask) for i in range(size)])


def dyn(x, start, size, axis):
    return lax.dynamic_slice_in_dim(x, start, size, axis)


def dot(a, b):
    return jnp.dot(a, b, preferred_element_type=F32)


def after(x, *others):
    return lax.optimization_barrier((x,) + others)[0]


def near(x, axis):
    return swap(x, axis, 1), swap(x, axis, 3)


def opposite(one, three, axis):
    half = one.shape[0] // 2
    return swap(one[:half], axis, 3), swap(three[half:], axis, 1)


def ring_gather(x, axis):
    one, three = near(x, axis)
    return [x, one, jnp.concatenate(opposite(one, three, axis)), three]


def in_order(blocks, index):
    laid = [lax.select_n(index ^ i, *blocks) for i in range(len(blocks))]
    return jnp.concatenate(laid)


def both(flag, first, second, axis=0):
    return jnp.where(
        flag == 0,
        jnp.concatenate([first, second], axis=axis),
        jnp.concatenate([second, first], axis=axis),
    )


def norm_kernel(place, tokens_ref, gain_ref, *out_refs):
    block = tokens_ref.shape[1] // 8
    values = tokens_ref[...].astype(F32)
    center = jnp.mean(values, axis=-1, keepdims=True)
    spread = jnp.mean(jnp.square(values - center), axis=-1, keepdims=True)
    scale = lax.rsqrt(spread + 1e-06)
    for relative in range(4):
        column = pl.multiple_of((place[1] * 4 + (place[2] ^ relative)) * block, 128)
        part = tokens_ref[:, pl.ds(column, block)].astype(F32)
        normed = ((part - center) * scale * gain_ref[:, pl.ds(column, block)]).astype(BF)
        out_refs[relative][...] = normed


def norm_rows(tokens, gain, place, count, piece):
    width = tokens.shape[1]
    block = width // 8
    out = jax.ShapeDtypeStruct((count * piece, block), BF)
    return pl.pallas_call(
        norm_kernel,
        grid_spec=pltpu.PrefetchScalarGridSpec(
            num_scalar_prefetch=1,
            grid=(count,),
            in_specs=[
                pl.BlockSpec((piece, width), lambda i, place: (i ^ place[0], 0)),
                pl.BlockSpec((1, width), lambda i, place: (0, 0)),
            ],
            out_specs=[pl.BlockSpec((piece, block), lambda i, place: (i, 0))] * 4,
        ),
        out_shape=[out] * 4,
        compiler_params=pltpu.CompilerParams(vmem_limit_bytes=32 * 2**20),
        cost_estimate=pl.CostEstimate(
            flops=8 * count * piece * width,
            bytes_accessed=3 * count * piece * width,
            transcendentals=0,
        ),
        name="norm_rows",
    )(place, tokens, gain.reshape(1, width))


def attend_kernel(q_ref, *refs):
    kv_refs, out_ref = refs[:-1], refs[-1]
    queries = q_ref[...]
    scores = [
        lax.dot_general(queries, kv[:, :HEAD], (((1,), (1,)), ((), ())), preferred_element_type=F32)
        for kv in kv_refs
    ]
    top = functools.reduce(jnp.maximum, [jnp.max(s, axis=-1, keepdims=True) for s in scores])
    factor = HEAD ** (-0.5) * LOG2E
    total, mixed = 0.0, 0.0
    for part, kv in zip(scores, kv_refs):
        weights = jnp.exp2((part - top) * factor)
        total = total + jnp.sum(weights, axis=-1, keepdims=True)
        mixed = mixed + dot(weights.astype(BF), kv[:, HEAD:])
    out_ref[...] = (mixed / total).astype(BF)


def attend(queries, kv_parts):
    rows = queries.shape[0]
    step = min(256, rows)
    keys = sum(part.shape[0] for part in kv_parts)
    return pl.pallas_call(
        attend_kernel,
        grid=(rows // step,),
        in_specs=[pl.BlockSpec((step, HEAD), lambda i: (i, 0))]
        + [pl.BlockSpec(part.shape, lambda i: (0, 0)) for part in kv_parts],
        out_specs=pl.BlockSpec((step, HEAD), lambda i: (i, 0)),
        out_shape=jax.ShapeDtypeStruct((rows, HEAD), BF),
        compiler_params=pltpu.CompilerParams(vmem_limit_bytes=48 * 2**20),
        cost_estimate=pl.CostEstimate(
            flops=4 * rows * keys * HEAD,
            bytes_accessed=4 * HEAD * (rows + keys),
            transcendentals=rows * keys,
        ),
        name="attend",
    )(queries, *kv_parts)


def on_device(
    tokens,
    norm_gain,
    qkv_weight,
    qk_gains,
    in_weight,
    in_bias,
    out_weight,
    mlp_out_weight,
    out_bias,
    targets,
):
    xh, z, xl, y, c = (lax.axis_index(a) for a in ("xh", "z", "xl", "y", "c"))
    rows, width = tokens.shape
    block = width // 8
    target_block = targets.shape[1] // 8
    piece = rows // 16
    half = rows // 2
    mine = (c * 4 + y) * 2 + xl

    by_head = qkv_weight.reshape(block, 3, 2, HEAD)
    qkv_w = both(xh, by_head[:, :, 0].reshape(block, 3 * HEAD), by_head[:, :, 1].reshape(block, 3 * HEAD), 1)
    qkv_w1, qkv_w3 = near(qkv_w, "z")

    give_norm = norm_rows(tokens, norm_gain, jnp.stack([mine, 1 - xh, z]), 2, piece)
    got = swap(jnp.concatenate(give_norm, axis=1), "xh")
    norm_own = norm_rows(tokens, norm_gain, jnp.stack([mine, xh, z]), 16, piece)
    around = ring_gather(got, "y")
    around = jnp.concatenate(around)
    beyond = swap(around, "c")
    norm_far = [
        jnp.concatenate([p[:, i * block : (i + 1) * block] for p in (around, beyond)]) for i in range(4)
    ]

    in_w = after(in_weight, qkv_w1, qkv_w3)
    qkv_w2 = jnp.concatenate(opposite(qkv_w1, qkv_w3, "z"))
    in_w1, in_w3 = near(in_w, "z")
    in_w2 = jnp.concatenate(opposite(in_w1, in_w3, "z"))
    qkv_ws, in_ws = (qkv_w, qkv_w1, qkv_w2, qkv_w3), (in_weight, in_w1, in_w2, in_w3)

    out_w = jnp.concatenate([out_weight, mlp_out_weight])
    far_w = swap(after(out_w, got), "xh")

    def own_head_first(w):
        return jnp.concatenate([both(xh, w[:HEAD], w[HEAD : 2 * HEAD]), w[2 * HEAD :]])

    base_rows = dyn(tokens, mine * piece, piece, 0).reshape(piece, 8, block)
    goal_rows = dyn(targets, mine * piece, piece, 0).reshape(piece, 8, target_block)
    spread_rows = jnp.concatenate([base_rows, goal_rows], axis=2).transpose(1, 0, 2)
    own_spread = lax.all_to_all(spread_rows, ("xh", "z"), split_axis=0, concat_axis=0, tiled=True)

    def project(parts, weights):
        order = (0, 1, 3, 2)
        return functools.reduce(jnp.add, [dot(parts[i], weights[i]) for i in order])

    qkv_own, qkv_far = project(norm_own, qkv_ws), project(norm_far, qkv_ws)
    own_head, other_head = slice(0, 3 * HEAD), slice(3 * HEAD, 6 * HEAD)
    give = jnp.concatenate([qkv_far[:, other_head], qkv_own[:, other_head]]).astype(BF)
    give = after(give, own_spread)
    keep = jnp.concatenate([qkv_own[:, own_head], qkv_far[:, own_head]])
    qkv = keep + swap(give, "xh").astype(F32)
    queries = layer_norm(qkv[:, :HEAD], qk_gains[0]).astype(BF)
    own_keys = layer_norm(qkv[:, HEAD : 2 * HEAD], qk_gains[1]).astype(BF)
    own_kv = jnp.concatenate([own_keys, qkv[:, 2 * HEAD :].astype(BF)], axis=1)
    kv_one, kv_three = near(own_kv, "z")
    kv_parts = [own_kv, kv_one, kv_three, *opposite(kv_one, kv_three, "z")]

    all_targets = lax.all_gather(own_spread[:, :, block:], ("xl", "y", "c"), axis=0, tiled=True)

    mlp_far = swap(project(norm_far, in_ws).astype(BF), "xh")
    mlp_input = project(norm_own, in_ws) + mlp_far.astype(F32)
    hidden = jax.nn.gelu(mlp_input + in_bias, approximate=False).astype(BF)
    hidden = ring_gather(hidden, "z")

    attended = attend(queries, kv_parts)
    attended = jnp.concatenate([attended[:rows], swap(attended[rows:], "xh")], axis=1)
    attended = after(attended, all_targets, far_w)
    attended = ring_gather(attended, "z")

    def half_rows(start):
        return jnp.concatenate(
            [jnp.concatenate([a[start : start + half], h[start : start + half]], axis=1) for a, h in zip(attended, hidden)]
        )

    keep_rows, give_rows = half_rows(0), half_rows(half)

    def over_core(w):
        got = swap(dot(give_rows, w).astype(BF), "c")
        return (dot(keep_rows, w) + got.astype(F32)).reshape(4, half, block)

    quarter = half // 4

    def chunks(x, start, count):
        return x[:, start * quarter : (start + count) * quarter]

    own_w, far_w = own_head_first(out_w), own_head_first(far_w)
    par, own = over_core(far_w), over_core(own_w)
    par_got = swap(chunks(par, 1, 2).astype(BF), "y", 1).astype(F32)
    own_got = swap(chunks(own, 2, 2).astype(BF), "y", 3).astype(F32)
    par_next = swap((chunks(par, 3, 1) + chunks(par_got, 1, 1)).astype(BF), "y", 3).astype(F32)
    own_next = swap((chunks(own, 1, 1) + chunks(own_got, 0, 1)).astype(BF), "y", 1).astype(F32)
    par_sum = chunks(par, 0, 1) + chunks(par_got, 0, 1) + par_next
    own_sum = chunks(own, 0, 1) + chunks(own_got, 1, 1) + own_next
    sums = jnp.concatenate([own_sum, par_sum], axis=2)
    sums = sums[:, :piece] + swap(sums[:, piece:].astype(BF), "xl").astype(F32)
    theirs = swap(sums[:, :, block:].astype(BF), "xh").astype(F32)
    sum_own = in_order([sums[i, :, :block] for i in range(4)], z)
    sum_theirs = in_order([theirs[i] for i in range(4)], z)
    total = both(xh, sum_own, sum_theirs)
    base = own_spread[:, :, :block].reshape(8 * piece, block).astype(F32)
    bias = dyn(out_bias, (xh * 4 + z) * block, block, 0)
    out_piece = (base + bias + total).astype(BF)

    turned = lax.ppermute(
        out_piece,
        ("xh", "z", "xl", "y"),
        [(a * 8 + b, b * 8 + a) for a in range(8) for b in range(8)],
    )
    narrow = block // 2
    stay = dyn(turned, c * narrow, narrow, 1)
    come = swap(dyn(turned, (1 - c) * narrow, narrow, 1), "c")
    own_columns = lax.all_gather(both(c, stay, come), ("xh", "z"), axis=0, tiled=True)

    total_tokens = rows * 8
    over_xl_pair = both(xl, out_piece, swap(out_piece, "xl"))
    by_place = own_columns.reshape(2, 4, 16 * piece, narrow)
    gram = 0.0
    for relative, part in enumerate(ring_gather(over_xl_pair, "y")):
        other = swap(part, "c")
        part, other = part.reshape(2, 8 * piece, block), other.reshape(2, 8 * piece, block)
        these = dyn(by_place, y ^ relative, 1, 1).reshape(2, 16 * piece, narrow)
        full = both(c, part, other, axis=1)
        gram = gram + jnp.einsum("ati,atj->ij", these, full, preferred_element_type=F32)
    all_targets = all_targets.reshape(total_tokens, target_block)
    cross = jnp.einsum("ti,tj->ij", own_columns, all_targets, preferred_element_type=F32)
    return gram / total_tokens, cross / total_tokens


def solution(mesh):
    fine = Mesh(mesh.devices.reshape(2, 4, 2, 4, 2), ("xh", "z", "xl", "y", "c"))
    dp, mp = ("xh", "z"), ("xl", "y", "c")
    placed = (
        P(dp, None),
        P(),
        P(dp, None, mp),
        P(),
        P(dp, mp),
        P(mp),
        P(mp, dp),
        P(mp, dp),
        P(),
        P(dp, None),
    )
    return jax.shard_map(
        on_device,
        mesh=fine,
        in_specs=placed,
        out_specs=(P(mp, dp), P(mp, dp)),
        check_vma=False,
    )
```

```python
import functools

import jax
import jax.numpy as jnp
from jax import lax
from jax.experimental import pallas as pl
from jax.experimental.pallas import tpu as pltpu
from jax.sharding import Mesh, PartitionSpec as P

HEAD = 128
BF = jnp.bfloat16
F32 = jnp.float32
LOG2E = 1.4426950408889634


def layer_norm(inputs, norm_scale):
    center = jnp.mean(inputs, axis=-1, keepdims=True)
    spread = jnp.mean(jnp.square(inputs - center), axis=-1, keepdims=True)
    return (inputs - center) * lax.rsqrt(spread + 1e-06) * norm_scale


def swap(x, axis, mask=1):
    size = lax.axis_size(axis)
    return lax.ppermute(x, axis, [(i, i ^ mask) for i in range(size)])


def dyn(x, start, size, axis):
    return lax.dynamic_slice_in_dim(x, start, size, axis)


def dot(a, b):
    return jnp.dot(a, b, preferred_element_type=F32)


def after(x, *others):
    return lax.optimization_barrier((x,) + others)[0]


def near(x, axis):
    return swap(x, axis, 1), swap(x, axis, 3)


def opposite(one, three, axis):
    half = one.shape[0] // 2
    return swap(one[:half], axis, 3), swap(three[half:], axis, 1)


def ring_gather(x, axis):
    one, three = near(x, axis)
    return [x, one, jnp.concatenate(opposite(one, three, axis)), three]


def in_order(blocks, index):
    laid = [lax.select_n(index ^ i, *blocks) for i in range(len(blocks))]
    return jnp.concatenate(laid)


def both(flag, first, second, axis=0):
    return jnp.where(
        flag == 0,
        jnp.concatenate([first, second], axis=axis),
        jnp.concatenate([second, first], axis=axis),
    )


def norm_kernel(place, tokens_ref, gain_ref, *out_refs):
    block = tokens_ref.shape[1] // 8
    values = tokens_ref[...].astype(F32)
    center = jnp.mean(values, axis=-1, keepdims=True)
    spread = jnp.mean(jnp.square(values - center), axis=-1, keepdims=True)
    scale = lax.rsqrt(spread + 1e-06)
    for relative in range(4):
        column = pl.multiple_of((place[1] * 4 + (place[2] ^ relative)) * block, 128)
        part = tokens_ref[:, pl.ds(column, block)].astype(F32)
        normed = ((part - center) * scale * gain_ref[:, pl.ds(column, block)]).astype(BF)
        out_refs[relative][...] = normed


def norm_rows(tokens, gain, place, count, piece):
    width = tokens.shape[1]
    block = width // 8
    out = jax.ShapeDtypeStruct((count * piece, block), BF)
    return pl.pallas_call(
        norm_kernel,
        grid_spec=pltpu.PrefetchScalarGridSpec(
            num_scalar_prefetch=1,
            grid=(count,),
            in_specs=[
                pl.BlockSpec((piece, width), lambda i, place: (i ^ place[0], 0)),
                pl.BlockSpec((1, width), lambda i, place: (0, 0)),
            ],
            out_specs=[pl.BlockSpec((piece, block), lambda i, place: (i, 0))] * 4,
        ),
        out_shape=[out] * 4,
        compiler_params=pltpu.CompilerParams(vmem_limit_bytes=24 * 2**20),
        name="norm_rows",
    )(place, tokens, gain.reshape(1, width))


def attend_kernel(q_ref, *refs):
    kv_refs, out_ref = refs[:-1], refs[-1]
    queries = q_ref[...]
    scores = [
        lax.dot_general(queries, kv[:, :HEAD], (((1,), (1,)), ((), ())), preferred_element_type=F32)
        for kv in kv_refs
    ]
    top = functools.reduce(jnp.maximum, [jnp.max(s, axis=-1, keepdims=True) for s in scores])
    factor = HEAD ** (-0.5) * LOG2E
    total, mixed = 0.0, 0.0
    for part, kv in zip(scores, kv_refs):
        weights = jnp.exp2((part - top) * factor)
        total = total + jnp.sum(weights, axis=-1, keepdims=True)
        mixed = mixed + dot(weights.astype(BF), kv[:, HEAD:])
    out_ref[...] = (mixed / total).astype(BF)


def attend(queries, kv_parts):
    rows = queries.shape[0]
    step = min(256, rows)
    keys = sum(part.shape[0] for part in kv_parts)
    return pl.pallas_call(
        attend_kernel,
        grid=(rows // step,),
        in_specs=[pl.BlockSpec((step, HEAD), lambda i: (i, 0))]
        + [pl.BlockSpec(part.shape, lambda i: (0, 0), pipeline_mode=pl.Buffered(1)) for part in kv_parts],
        out_specs=pl.BlockSpec((step, HEAD), lambda i: (i, 0)),
        out_shape=jax.ShapeDtypeStruct((rows, HEAD), BF),
        compiler_params=pltpu.CompilerParams(vmem_limit_bytes=24 * 2**20),
        name="attend",
    )(queries, *kv_parts)


def pieces_dot(parts, weights, part=None):
    w0, w1, low, high, w3 = weights
    n0, n1, n2, n3 = parts
    half = n2.shape[1] // 2
    pairs = [(n0[...], w0), (n1[...], w1), (n3[...], w3), (n2[:, :half], low), (n2[:, half:], high)]
    total = None
    for rows, w in pairs:
        term = dot(rows, w[...] if part is None else w[part])
        total = term if total is None else total + term
    return total


def qkv_kernel(place, *refs):
    own, far, weights = refs[0:4], refs[4:8], refs[8:13]
    give_ref, keep_ref, hold = refs[13:]
    rows = own[0].shape[0]
    hold[:rows] = pieces_dot(own, weights, 0)
    hold[rows:] = pieces_dot(far, weights, 0)
    mine = pl.ds(pl.multiple_of(place[0] * HEAD, HEAD), HEAD)
    other = pl.ds(pl.multiple_of((1 - place[0]) * HEAD, HEAD), HEAD)
    keep_ref[...] = hold[:, mine]
    give_ref[:rows] = hold[rows:, other].astype(BF)
    give_ref[rows:] = hold[:rows, other].astype(BF)


def project_qkv(own, far, weights, xh):
    rows, block = own[0].shape

    def whole(x):
        return pl.BlockSpec(x.shape, lambda i, place: (0, 0), pipeline_mode=pl.Buffered(1))

    def third(w):
        return pl.BlockSpec((1,) + w.shape[1:], lambda i, place: (i, 0, 0))

    column = pl.BlockSpec((2 * rows, HEAD), lambda i, place: (0, i))
    return pl.pallas_call(
        qkv_kernel,
        grid_spec=pltpu.PrefetchScalarGridSpec(
            num_scalar_prefetch=1,
            grid=(3,),
            in_specs=[whole(x) for x in (*own, *far)] + [third(w) for w in weights],
            out_specs=[column, column],
            scratch_shapes=[pltpu.VMEM((2 * rows, 2 * HEAD), F32)],
        ),
        out_shape=[
            jax.ShapeDtypeStruct((2 * rows, 3 * HEAD), BF),
            jax.ShapeDtypeStruct((2 * rows, 3 * HEAD), F32),
        ],
        compiler_params=pltpu.CompilerParams(vmem_limit_bytes=32 * 2**20),
        name="project_qkv",
    )(jnp.reshape(xh, (1,)), *own, *far, *weights)


def mlp_kernel(*refs):
    refs[9][...] = pieces_dot(refs[0:4], refs[4:9]).astype(refs[9].dtype)


def project_mlp(parts, weights, dtype):
    rows, block = parts[0].shape
    wide = weights[0].shape[1]
    step = wide // 3
    return pl.pallas_call(
        mlp_kernel,
        grid=(3,),
        in_specs=[pl.BlockSpec(x.shape, lambda i: (0, 0), pipeline_mode=pl.Buffered(1)) for x in parts]
        + [pl.BlockSpec((w.shape[0], step), lambda i: (0, i)) for w in weights],
        out_specs=pl.BlockSpec((rows, step), lambda i: (0, i)),
        out_shape=jax.ShapeDtypeStruct((rows, wide), dtype),
        compiler_params=pltpu.CompilerParams(vmem_limit_bytes=48 * 2**20),
        name="project_mlp",
    )(*parts, *weights)


def output_kernel(place, *refs):
    attended, hidden, w_ref, out_ref = refs[0:4], refs[4:8], refs[8], refs[9]
    first = w_ref[0, pl.ds(pl.multiple_of(place[0] * HEAD, HEAD), HEAD)]
    second = w_ref[0, pl.ds(pl.multiple_of((1 - place[0]) * HEAD, HEAD), HEAD)]
    heads = jnp.concatenate([first, second])
    for i in range(4):
        a, h = attended[i], hidden[i]
        total = dot(h[...], w_ref[0, 2 * HEAD :]) + dot(a[...], heads)
        out_ref[0, i] = total.astype(out_ref.dtype)


def project_out(attended, hidden, which, weights, xh, dtype):
    rows = hidden[2].shape[0]
    _, depth, block = weights.shape
    step = block // 3

    def rows_of(x):
        at = 0 if x.shape[0] == rows else which
        return pl.BlockSpec((rows, x.shape[1]), lambda side, i, place: (at, 0), pipeline_mode=pl.Buffered(1))

    return pl.pallas_call(
        output_kernel,
        grid_spec=pltpu.PrefetchScalarGridSpec(
            num_scalar_prefetch=1,
            grid=(2, 3),
            in_specs=[rows_of(x) for x in (*attended, *hidden)]
            + [pl.BlockSpec((1, depth, step), lambda side, i, place: (side, 0, i))],
            out_specs=pl.BlockSpec((1, 4, rows, step), lambda side, i, place: (side, 0, 0, i)),
        ),
        out_shape=jax.ShapeDtypeStruct((2, 4, rows, block), dtype),
        compiler_params=pltpu.CompilerParams(vmem_limit_bytes=60 * 2**20),
        name="project_out",
    )(jnp.reshape(xh, (1,)), *attended, *hidden, weights)


def moment_kernel(total_tokens, place, *refs):
    columns, parts, others = refs[0:5], refs[5:10], refs[10:15]
    gram_ref, cross_ref, hold = refs[15:]
    tokens_here = hold.shape[3] // 2
    index = pl.program_id(0)

    @pl.when(index == 0)
    def _():
        for relative, ref in ((0, columns[0]), (1, columns[1]), (3, columns[4])):
            for side in range(2):
                rows = ref[side * 2 * tokens_here : (side + 1) * 2 * tokens_here]
                hold[relative ^ place[0], side ^ place[1]] = rows.T
        for side in range(2):
            hold[2 ^ place[0], side ^ place[1]] = columns[2 + side][...].T

    def part_rows(refs, relative, side):
        if relative == 2:
            return refs[2 + side][...]
        ref = refs[relative if relative < 2 else 4]
        return ref[side * tokens_here : (side + 1) * tokens_here]

    total = None
    for relative in range(4):
        for side in range(2):
            full = jnp.concatenate([part_rows(parts, relative, side), part_rows(others, relative, side)])
            term = dot(hold[relative, side], full)
            total = term if total is None else total + term
    total = total / total_tokens

    @pl.when(index < pl.num_programs(0) - 1)
    def _():
        gram_ref[...] = total

    @pl.when(index == pl.num_programs(0) - 1)
    def _():
        cross_ref[...] = total


def moments(columns, parts, others, place, block, total_tokens):
    narrow = columns[0].shape[1]
    step = parts[0].shape[1] - block
    steps = block // step
    kernel = functools.partial(moment_kernel, total_tokens)

    def whole(x):
        return pl.BlockSpec(x.shape, lambda i, place: (0, 0), pipeline_mode=pl.Buffered(1))

    def column(x):
        return pl.BlockSpec((x.shape[0], step), lambda i, place: (0, i))

    return pl.pallas_call(
        kernel,
        grid_spec=pltpu.PrefetchScalarGridSpec(
            num_scalar_prefetch=1,
            grid=(steps + 1,),
            in_specs=[whole(x) for x in columns] + [column(x) for x in (*parts, *others)],
            out_specs=[
                pl.BlockSpec((narrow, step), lambda i, place: (0, jnp.minimum(i, steps - 1))),
                pl.BlockSpec((narrow, step), lambda i, place: (0, 0)),
            ],
            scratch_shapes=[pltpu.VMEM((4, 2, narrow, columns[2].shape[0]), BF)],
        ),
        out_shape=[
            jax.ShapeDtypeStruct((narrow, block), F32),
            jax.ShapeDtypeStruct((narrow, step), F32),
        ],
        compiler_params=pltpu.CompilerParams(vmem_limit_bytes=60 * 2**20),
        name="moments",
    )(place, *columns, *parts, *others)


def on_device(
    tokens,
    norm_gain,
    qkv_weight,
    qk_gains,
    in_weight,
    in_bias,
    out_weight,
    mlp_out_weight,
    out_bias,
    targets,
):
    xh, z, xl, y, c = (lax.axis_index(a) for a in ("xh", "z", "xl", "y", "c"))
    rows, width = tokens.shape
    block = width // 8
    target_block = targets.shape[1] // 8
    piece = rows // 16
    half = rows // 2
    mine = (c * 4 + y) * 2 + xl

    qkv_w = qkv_weight.transpose(1, 0, 2)
    qkv_w1, qkv_w3 = near(qkv_w, "z")

    share = 2 * piece
    first_rows = dyn(tokens, (c * 4 + y) * share, share, 0)
    give_norm = norm_rows(first_rows, norm_gain, jnp.stack([xl, 1 - xh, z]), 2, piece)
    give_norm = jnp.concatenate(give_norm, axis=1)
    got = swap(give_norm, "xh")
    norm_own = norm_rows(after(tokens, give_norm), norm_gain, jnp.stack([mine, xh, z]), 16, piece)

    out_raw, got, *norm_own = lax.optimization_barrier((out_weight, got, *norm_own))
    depth = mlp_out_weight.shape[0] // 3
    mlp_raws = [mlp_out_weight[i * depth : (i + 1) * depth] for i in range(3)]
    far_ws = [swap(out_raw, "xh")]
    got_one, got_three = near(got, "y")
    got_one, got_three, qkv_w1, qkv_w3, far_ws[0], mlp_raws[0] = lax.optimization_barrier(
        (got_one, got_three, qkv_w1, qkv_w3, far_ws[0], mlp_raws[0])
    )
    far_ws.append(swap(mlp_raws[0], "xh"))
    middle = block // 2
    qkv_low = swap(qkv_w1[:, :middle], "z", 3)
    qkv_high = swap(qkv_w3[:, middle:], "z", 1)
    got_low, got_high = opposite(got_one, got_three, "y")
    got_low, got_high, qkv_low, qkv_high, in_raw, far_ws[1], mlp_raws[1] = lax.optimization_barrier(
        (got_low, got_high, qkv_low, qkv_high, in_weight, far_ws[1], mlp_raws[1])
    )
    far_ws.append(swap(mlp_raws[1], "xh"))
    around = jnp.concatenate([got, got_one, got_low, got_high, got_three])
    beyond = swap(around, "c")
    in_w1, in_w3 = near(in_raw, "z")
    norm_far = [
        jnp.concatenate([p[:, i * block : (i + 1) * block] for p in (around, beyond)]) for i in range(4)
    ]

    give, keep = project_qkv(norm_own, norm_far, (qkv_w, qkv_w1, qkv_low, qkv_high, qkv_w3), xh)
    give, far_ws[2] = lax.optimization_barrier((give, far_ws[2]))
    taken = swap(give, "xh")
    in_w1, in_w3, *norms = lax.optimization_barrier((in_w1, in_w3, *norm_own, *norm_far, give))
    norm_own, norm_far = norms[:4], norms[4:8]
    in_first, in_last = in_w1[:middle], in_w3[middle:]
    in_low, in_high = swap(in_first, "z", 3), swap(in_last, "z", 1)
    taken = after(taken, in_first, in_last)
    qkv = keep + taken.astype(F32)
    queries = layer_norm(qkv[:, :HEAD], qk_gains[0]).astype(BF)
    own_keys = layer_norm(qkv[:, HEAD : 2 * HEAD], qk_gains[1]).astype(BF)
    own_kv = jnp.concatenate([own_keys, qkv[:, 2 * HEAD :].astype(BF)], axis=1)
    kv_one, kv_three = near(own_kv, "z")

    in_ws = (in_weight, in_w1, in_low, in_high, in_w3)
    mlp_give = project_mlp(norm_far, in_ws, BF)
    mlp_far = swap(mlp_give, "xh")
    mlp_give, *norm_own = lax.optimization_barrier((mlp_give, *norm_own))
    mlp_own = project_mlp(norm_own, in_ws, F32)
    mlp_own, kv_one, kv_three = lax.optimization_barrier((mlp_own, kv_one, kv_three))
    kv_low, kv_high = opposite(kv_one, kv_three, "z")
    mlp_far, kv_low, kv_high = lax.optimization_barrier((mlp_far, kv_low, kv_high))
    kv_parts = [own_kv, kv_one, kv_three, kv_low, kv_high]
    mlp_input = mlp_own + mlp_far.astype(F32)
    hidden = jax.nn.gelu(mlp_input + in_bias, approximate=False).astype(BF)
    hidden, queries, mlp_raws[2] = lax.optimization_barrier((hidden, queries, mlp_raws[2]))
    far_ws.append(swap(mlp_raws[2], "xh"))
    hid_one, hid_three = near(hidden, "z")

    attended = attend(queries, kv_parts)
    attended, hid_one, hid_three, far_ws[3] = lax.optimization_barrier((attended, hid_one, hid_three, far_ws[3]))
    out_ws = jnp.stack([jnp.concatenate([out_weight, mlp_out_weight]), jnp.concatenate(far_ws)])
    hid_low, hid_high = opposite(hid_one, hid_three, "z")
    attended = jnp.concatenate([attended[:rows], swap(attended[rows:], "xh")], axis=1)
    att_one, att_three = near(attended, "z")
    att_two = swap(attended, "z", 2)

    att_one, att_two, att_three, hid_low, hid_high, out_ws = lax.optimization_barrier(
        (att_one, att_two, att_three, hid_low, hid_high, out_ws)
    )
    att_parts = (attended, att_one, att_two, att_three)
    hid_keep, hid_give = (hidden, hid_one, hid_low, hid_three), (hidden, hid_one, hid_high, hid_three)

    got_sums = swap(project_out(att_parts, hid_give, 1, out_ws, xh, BF), "c")
    got_sums, raw_tokens, raw_targets = lax.optimization_barrier((got_sums, tokens, targets))

    base_rows = dyn(raw_tokens, mine * piece, piece, 0).reshape(piece, 8, block)
    goal_rows = dyn(raw_targets, mine * piece, piece, 0).reshape(piece, 8, target_block)
    spread_rows = jnp.concatenate([base_rows, goal_rows], axis=2).transpose(1, 0, 2)
    own_spread = lax.all_to_all(spread_rows, ("xh", "z"), split_axis=0, concat_axis=0, tiled=True)
    sums = project_out(att_parts, hid_keep, 0, out_ws, xh, BF)
    own, par = [sums[i].astype(F32) + got_sums[i].astype(F32) for i in range(2)]

    quarter = half // 4

    def chunks(x, start, count):
        return x[:, start * quarter : (start + count) * quarter]

    par_got = swap(chunks(par, 1, 2).astype(BF), "y", 1)
    own_got = swap(chunks(own, 2, 2).astype(BF), "y", 3)
    par_got, own_got, own_spread = lax.optimization_barrier((par_got, own_got, own_spread))
    base = own_spread[:, :, :block].reshape(8 * piece, block)
    own_goals = own_spread[:, :, block:].reshape(8 * piece, target_block)
    par_next = swap((chunks(par, 3, 1) + chunks(par_got, 1, 1).astype(F32)).astype(BF), "y", 3).astype(F32)
    own_next = swap((chunks(own, 1, 1) + chunks(own_got, 0, 1).astype(F32)).astype(BF), "y", 1).astype(F32)
    par_sum = chunks(par, 0, 1) + chunks(par_got, 0, 1).astype(F32) + par_next
    own_sum = chunks(own, 0, 1) + chunks(own_got, 1, 1).astype(F32) + own_next
    sums = jnp.concatenate([own_sum, par_sum], axis=2)
    sums = sums[:, :piece] + swap(sums[:, piece:].astype(BF), "xl").astype(F32)
    theirs = swap(sums[:, :, block:].astype(BF), "xh").astype(F32)
    sum_own = in_order([sums[i, :, :block] for i in range(4)], z)
    sum_theirs = in_order([theirs[i] for i in range(4)], z)
    total = both(xh, sum_own, sum_theirs)
    bias = dyn(out_bias, (xh * 4 + z) * block, block, 0)
    out_piece = (base.astype(F32) + bias + total).astype(BF)

    narrow = block // 2

    stay, leave = dyn(out_piece, c * narrow, narrow, 1), dyn(out_piece, (1 - c) * narrow, narrow, 1)
    pair = jnp.concatenate([stay, swap(leave, "c")])
    beside = jnp.concatenate([out_piece, own_goals], axis=1)
    over_xl = swap(beside, "xl")
    pair = lax.ppermute(
        pair,
        ("xh", "z", "xl", "y"),
        [(a * 8 + b, b * 8 + a) for a in range(8) for b in range(8)],
    )
    pair, over_xl = lax.optimization_barrier((pair, over_xl))
    over_xl_pair = jnp.concatenate([beside, over_xl])
    part_one, part_three = near(over_xl_pair, "y")
    pair = jnp.concatenate([pair, swap(pair, "xh")])
    col_one, col_three = near(pair, "z")
    col_one, col_three, part_one, part_three = lax.optimization_barrier((col_one, col_three, part_one, part_three))
    col_low, col_high = opposite(col_one, col_three, "z")
    part_low, part_high = opposite(part_one, part_three, "y")
    col_low, col_high, part_low, part_high = lax.optimization_barrier((col_low, col_high, part_low, part_high))
    columns = [pair, col_one, col_low, col_high, col_three]
    parts = [over_xl_pair, part_one, part_low, part_high, part_three]
    others = [swap(part, "c") for part in parts]
    return moments(columns, parts, others, jnp.stack([y ^ z, xh ^ xl]), block, rows * 8)


def solution(mesh):
    fine = Mesh(mesh.devices.reshape(2, 4, 2, 4, 2), ("xh", "z", "xl", "y", "c"))
    dp, mp = ("xh", "z"), ("xl", "y", "c")
    placed = (
        P(dp, None),
        P(),
        P(dp, None, mp),
        P(),
        P(dp, mp),
        P(mp),
        P(mp, dp),
        P(mp, dp),
        P(),
        P(dp, None),
    )
    return jax.shard_map(
        on_device,
        mesh=fine,
        in_specs=placed,
        out_specs=(P(mp, dp), P(mp, dp)),
        check_vma=False,
    )
```

```python
import functools

import jax
import jax.numpy as jnp
from jax import lax
from jax.experimental import pallas as pl
from jax.experimental.pallas import tpu as pltpu
from jax.sharding import Mesh, PartitionSpec as P

HEAD = 128
BF = jnp.bfloat16
F32 = jnp.float32
LOG2E = 1.4426950408889634


def layer_norm(inputs, norm_scale):
    center = jnp.mean(inputs, axis=-1, keepdims=True)
    spread = jnp.mean(jnp.square(inputs - center), axis=-1, keepdims=True)
    return (inputs - center) * lax.rsqrt(spread + 1e-06) * norm_scale


def swap(x, axis, mask=1):
    size = lax.axis_size(axis)
    return lax.ppermute(x, axis, [(i, i ^ mask) for i in range(size)])


def dyn(x, start, size, axis):
    return lax.dynamic_slice_in_dim(x, start, size, axis)


def dot(a, b):
    return jnp.dot(a, b, preferred_element_type=F32)


def after(x, *others):
    return lax.optimization_barrier((x,) + others)[0]


def near(x, axis):
    return swap(x, axis, 1), swap(x, axis, 3)


def opposite(one, three, axis):
    half = one.shape[0] // 2
    return swap(one[:half], axis, 3), swap(three[half:], axis, 1)


def ring_gather(x, axis):
    one, three = near(x, axis)
    return [x, one, jnp.concatenate(opposite(one, three, axis)), three]


def in_order(blocks, index):
    laid = [lax.select_n(index ^ i, *blocks) for i in range(len(blocks))]
    return jnp.concatenate(laid)


def both(flag, first, second, axis=0):
    return jnp.where(
        flag == 0,
        jnp.concatenate([first, second], axis=axis),
        jnp.concatenate([second, first], axis=axis),
    )


def norm_kernel(place, tokens_ref, gain_ref, *out_refs):
    block = tokens_ref.shape[1] // 8
    values = tokens_ref[...].astype(F32)
    center = jnp.mean(values, axis=-1, keepdims=True)
    spread = jnp.mean(jnp.square(values - center), axis=-1, keepdims=True)
    scale = lax.rsqrt(spread + 1e-06)
    for relative in range(4):
        column = pl.multiple_of((place[1] * 4 + (place[2] ^ relative)) * block, 128)
        part = tokens_ref[:, pl.ds(column, block)].astype(F32)
        normed = ((part - center) * scale * gain_ref[:, pl.ds(column, block)]).astype(BF)
        out_refs[relative][...] = normed


def norm_rows(tokens, gain, place, count, piece):
    width = tokens.shape[1]
    block = width // 8
    out = jax.ShapeDtypeStruct((count * piece, block), BF)
    return pl.pallas_call(
        norm_kernel,
        grid_spec=pltpu.PrefetchScalarGridSpec(
            num_scalar_prefetch=1,
            grid=(count,),
            in_specs=[
                pl.BlockSpec((piece, width), lambda i, place: (i ^ place[0], 0)),
                pl.BlockSpec((1, width), lambda i, place: (0, 0)),
            ],
            out_specs=[pl.BlockSpec((piece, block), lambda i, place: (i, 0))] * 4,
        ),
        out_shape=[out] * 4,
        compiler_params=pltpu.CompilerParams(vmem_limit_bytes=24 * 2**20),
        name="norm_rows",
    )(place, tokens, gain.reshape(1, width))


def attend_kernel(q_ref, *refs):
    kv_refs, out_ref = refs[:-1], refs[-1]
    queries = q_ref[...]
    scores = [
        lax.dot_general(queries, kv[:, :HEAD], (((1,), (1,)), ((), ())), preferred_element_type=F32)
        for kv in kv_refs
    ]
    top = functools.reduce(jnp.maximum, [jnp.max(s, axis=-1, keepdims=True) for s in scores])
    factor = HEAD ** (-0.5) * LOG2E
    total, mixed = 0.0, 0.0
    for part, kv in zip(scores, kv_refs):
        weights = jnp.exp2((part - top) * factor)
        total = total + jnp.sum(weights, axis=-1, keepdims=True)
        mixed = mixed + dot(weights.astype(BF), kv[:, HEAD:])
    out_ref[...] = (mixed / total).astype(BF)


def attend(queries, kv_parts):
    rows = queries.shape[0]
    step = min(256, rows)
    keys = sum(part.shape[0] for part in kv_parts)
    return pl.pallas_call(
        attend_kernel,
        grid=(rows // step,),
        in_specs=[pl.BlockSpec((step, HEAD), lambda i: (i, 0))]
        + [pl.BlockSpec(part.shape, lambda i: (0, 0), pipeline_mode=pl.Buffered(1)) for part in kv_parts],
        out_specs=pl.BlockSpec((step, HEAD), lambda i: (i, 0)),
        out_shape=jax.ShapeDtypeStruct((rows, HEAD), BF),
        compiler_params=pltpu.CompilerParams(vmem_limit_bytes=24 * 2**20),
        name="attend",
    )(queries, *kv_parts)


def pieces_dot(parts, weights, part=None):
    w0, w1, low, high, w3 = weights
    n0, n1, n2, n3 = parts
    half = n2.shape[1] // 2
    pairs = [(n0[...], w0), (n1[...], w1), (n3[...], w3), (n2[:, :half], low), (n2[:, half:], high)]
    total = None
    for rows, w in pairs:
        term = dot(rows, w[...] if part is None else w[part])
        total = term if total is None else total + term
    return total


def qkv_kernel(place, *refs):
    own, far, weights = refs[0:4], refs[4:8], refs[8:13]
    give_ref, keep_ref, hold = refs[13:]
    rows = own[0].shape[0]
    hold[:rows] = pieces_dot(own, weights, 0)
    hold[rows:] = pieces_dot(far, weights, 0)
    mine = pl.ds(pl.multiple_of(place[0] * HEAD, HEAD), HEAD)
    other = pl.ds(pl.multiple_of((1 - place[0]) * HEAD, HEAD), HEAD)
    keep_ref[...] = hold[:, mine]
    give_ref[:rows] = hold[rows:, other].astype(BF)
    give_ref[rows:] = hold[:rows, other].astype(BF)


def project_qkv(own, far, weights, xh):
    rows, block = own[0].shape

    def whole(x):
        return pl.BlockSpec(x.shape, lambda i, place: (0, 0), pipeline_mode=pl.Buffered(1))

    def third(w):
        return pl.BlockSpec((1,) + w.shape[1:], lambda i, place: (i, 0, 0))

    column = pl.BlockSpec((2 * rows, HEAD), lambda i, place: (0, i))
    return pl.pallas_call(
        qkv_kernel,
        grid_spec=pltpu.PrefetchScalarGridSpec(
            num_scalar_prefetch=1,
            grid=(3,),
            in_specs=[whole(x) for x in (*own, *far)] + [third(w) for w in weights],
            out_specs=[column, column],
            scratch_shapes=[pltpu.VMEM((2 * rows, 2 * HEAD), F32)],
        ),
        out_shape=[
            jax.ShapeDtypeStruct((2 * rows, 3 * HEAD), BF),
            jax.ShapeDtypeStruct((2 * rows, 3 * HEAD), F32),
        ],
        compiler_params=pltpu.CompilerParams(vmem_limit_bytes=32 * 2**20),
        name="project_qkv",
    )(jnp.reshape(xh, (1,)), *own, *far, *weights)


def mlp_kernel(*refs):
    refs[9][...] = pieces_dot(refs[0:4], refs[4:9]).astype(refs[9].dtype)


def project_mlp(parts, weights, dtype):
    rows, block = parts[0].shape
    wide = weights[0].shape[1]
    step = wide // 3
    return pl.pallas_call(
        mlp_kernel,
        grid=(3,),
        in_specs=[pl.BlockSpec(x.shape, lambda i: (0, 0), pipeline_mode=pl.Buffered(1)) for x in parts]
        + [pl.BlockSpec((w.shape[0], step), lambda i: (0, i)) for w in weights],
        out_specs=pl.BlockSpec((rows, step), lambda i: (0, i)),
        out_shape=jax.ShapeDtypeStruct((rows, wide), dtype),
        compiler_params=pltpu.CompilerParams(vmem_limit_bytes=48 * 2**20),
        name="project_mlp",
    )(*parts, *weights)


def output_kernel(place, *refs):
    attended, hidden, w_ref, out_ref = refs[0:4], refs[4:8], refs[8], refs[9]
    first = w_ref[0, pl.ds(pl.multiple_of(place[0] * HEAD, HEAD), HEAD)]
    second = w_ref[0, pl.ds(pl.multiple_of((1 - place[0]) * HEAD, HEAD), HEAD)]
    heads = jnp.concatenate([first, second])
    for i in range(4):
        a, h = attended[i], hidden[i]
        total = dot(h[...], w_ref[0, 2 * HEAD :]) + dot(a[...], heads)
        out_ref[0, i] = total.astype(out_ref.dtype)


def project_out(attended, hidden, which, weights, xh, dtype):
    rows = hidden[2].shape[0]
    _, depth, block = weights.shape
    step = block // 3

    def rows_of(x):
        at = 0 if x.shape[0] == rows else which
        return pl.BlockSpec((rows, x.shape[1]), lambda side, i, place: (at, 0), pipeline_mode=pl.Buffered(1))

    return pl.pallas_call(
        output_kernel,
        grid_spec=pltpu.PrefetchScalarGridSpec(
            num_scalar_prefetch=1,
            grid=(2, 3),
            in_specs=[rows_of(x) for x in (*attended, *hidden)]
            + [pl.BlockSpec((1, depth, step), lambda side, i, place: (side, 0, i))],
            out_specs=pl.BlockSpec((1, 4, rows, step), lambda side, i, place: (side, 0, 0, i)),
        ),
        out_shape=jax.ShapeDtypeStruct((2, 4, rows, block), dtype),
        compiler_params=pltpu.CompilerParams(vmem_limit_bytes=60 * 2**20),
        name="project_out",
    )(jnp.reshape(xh, (1,)), *attended, *hidden, weights)


def moment_kernel(total_tokens, place, *refs):
    columns, parts, others = refs[0:5], refs[5:10], refs[10:15]
    gram_ref, cross_ref, hold = refs[15:]
    tokens_here = hold.shape[3] // 2
    index = pl.program_id(0)

    @pl.when(index == 0)
    def _():
        for relative, ref in ((0, columns[0]), (1, columns[1]), (3, columns[4])):
            for side in range(2):
                rows = ref[side * 2 * tokens_here : (side + 1) * 2 * tokens_here]
                hold[relative ^ place[0], side ^ place[1]] = rows.T
        for side in range(2):
            hold[2 ^ place[0], side ^ place[1]] = columns[2 + side][...].T

    def part_rows(refs, relative, side):
        if relative == 2:
            return refs[2 + side][...]
        ref = refs[relative if relative < 2 else 4]
        return ref[side * tokens_here : (side + 1) * tokens_here]

    total = None
    for relative in range(4):
        for side in range(2):
            full = jnp.concatenate([part_rows(parts, relative, side), part_rows(others, relative, side)])
            term = dot(hold[relative, side], full)
            total = term if total is None else total + term
    total = total / total_tokens

    @pl.when(index < pl.num_programs(0) - 1)
    def _():
        gram_ref[...] = total

    @pl.when(index == pl.num_programs(0) - 1)
    def _():
        cross_ref[...] = total


def moments(columns, parts, others, place, block, total_tokens):
    narrow = columns[0].shape[1]
    step = parts[0].shape[1] - block
    steps = block // step
    kernel = functools.partial(moment_kernel, total_tokens)

    def whole(x):
        return pl.BlockSpec(x.shape, lambda i, place: (0, 0), pipeline_mode=pl.Buffered(1))

    def column(x):
        return pl.BlockSpec((x.shape[0], step), lambda i, place: (0, i))

    return pl.pallas_call(
        kernel,
        grid_spec=pltpu.PrefetchScalarGridSpec(
            num_scalar_prefetch=1,
            grid=(steps + 1,),
            in_specs=[whole(x) for x in columns] + [column(x) for x in (*parts, *others)],
            out_specs=[
                pl.BlockSpec((narrow, step), lambda i, place: (0, jnp.minimum(i, steps - 1))),
                pl.BlockSpec((narrow, step), lambda i, place: (0, 0)),
            ],
            scratch_shapes=[pltpu.VMEM((4, 2, narrow, columns[2].shape[0]), BF)],
        ),
        out_shape=[
            jax.ShapeDtypeStruct((narrow, block), F32),
            jax.ShapeDtypeStruct((narrow, step), F32),
        ],
        compiler_params=pltpu.CompilerParams(vmem_limit_bytes=60 * 2**20),
        name="moments",
    )(place, *columns, *parts, *others)


def on_device(
    tokens,
    norm_gain,
    qkv_weight,
    qk_gains,
    in_weight,
    in_bias,
    out_weight,
    mlp_out_weight,
    out_bias,
    targets,
):
    xh, z, xl, y, c = (lax.axis_index(a) for a in ("xh", "z", "xl", "y", "c"))
    rows, width = tokens.shape
    block = width // 8
    target_block = targets.shape[1] // 8
    piece = rows // 16
    half = rows // 2
    mine = (c * 4 + y) * 2 + xl

    qkv_w = qkv_weight.transpose(1, 0, 2)
    qkv_w1, qkv_w3 = near(qkv_w, "z")

    share = 2 * piece
    first_rows = dyn(tokens, (c * 4 + y) * share, share, 0)
    give_norm = norm_rows(first_rows, norm_gain, jnp.stack([xl, 1 - xh, z]), 2, piece)
    give_norm = jnp.concatenate(give_norm, axis=1)
    got = swap(give_norm, "xh")
    norm_own = norm_rows(after(tokens, give_norm), norm_gain, jnp.stack([mine, xh, z]), 16, piece)

    out_raw, got, *norm_own = lax.optimization_barrier((out_weight, got, *norm_own))
    depth = mlp_out_weight.shape[0] // 3
    mlp_raws = [mlp_out_weight[i * depth : (i + 1) * depth] for i in range(3)]
    far_ws = [swap(out_raw, "xh")]
    got_one, got_three = near(got, "y")
    got_one, got_three, qkv_w1, qkv_w3, far_ws[0], mlp_raws[0] = lax.optimization_barrier(
        (got_one, got_three, qkv_w1, qkv_w3, far_ws[0], mlp_raws[0])
    )
    far_ws.append(swap(mlp_raws[0], "xh"))
    middle = block // 2
    qkv_low = swap(qkv_w1[:, :middle], "z", 3)
    qkv_high = swap(qkv_w3[:, middle:], "z", 1)
    got_low, got_high = opposite(got_one, got_three, "y")
    got_low, got_high, qkv_low, qkv_high, in_raw, far_ws[1], mlp_raws[1] = lax.optimization_barrier(
        (got_low, got_high, qkv_low, qkv_high, in_weight, far_ws[1], mlp_raws[1])
    )
    far_ws.append(swap(mlp_raws[1], "xh"))
    around = jnp.concatenate([got, got_one, got_low, got_high, got_three])
    beyond = swap(around, "c")
    in_w1, in_w3 = near(in_raw, "z")
    norm_far = [
        jnp.concatenate([p[:, i * block : (i + 1) * block] for p in (around, beyond)]) for i in range(4)
    ]

    give, keep = project_qkv(norm_own, norm_far, (qkv_w, qkv_w1, qkv_low, qkv_high, qkv_w3), xh)
    give, far_ws[2] = lax.optimization_barrier((give, far_ws[2]))
    taken = swap(give, "xh")
    in_w1, in_w3, *norms = lax.optimization_barrier((in_w1, in_w3, *norm_own, *norm_far, give))
    norm_own, norm_far = norms[:4], norms[4:8]
    in_first, in_last = in_w1[:middle], in_w3[middle:]
    in_low, in_high = swap(in_first, "z", 3), swap(in_last, "z", 1)
    taken = after(taken, in_first, in_last)
    qkv = keep + taken.astype(F32)
    queries = layer_norm(qkv[:, :HEAD], qk_gains[0]).astype(BF)
    own_keys = layer_norm(qkv[:, HEAD : 2 * HEAD], qk_gains[1]).astype(BF)
    own_kv = jnp.concatenate([own_keys, qkv[:, 2 * HEAD :].astype(BF)], axis=1)
    kv_one, kv_three = near(own_kv, "z")

    in_ws = (in_weight, in_w1, in_low, in_high, in_w3)
    mlp_give = project_mlp(norm_far, in_ws, BF)
    mlp_far = swap(mlp_give, "xh")
    mlp_give, *norm_own = lax.optimization_barrier((mlp_give, *norm_own))
    mlp_own = project_mlp(norm_own, in_ws, F32)
    mlp_own, kv_one, kv_three = lax.optimization_barrier((mlp_own, kv_one, kv_three))
    kv_low, kv_high = opposite(kv_one, kv_three, "z")
    mlp_far, kv_low, kv_high = lax.optimization_barrier((mlp_far, kv_low, kv_high))
    kv_parts = [own_kv, kv_one, kv_three, kv_low, kv_high]
    mlp_input = mlp_own + mlp_far.astype(F32)
    hidden = jax.nn.gelu(mlp_input + in_bias, approximate=False).astype(BF)
    hidden, queries, mlp_raws[2] = lax.optimization_barrier((hidden, queries, mlp_raws[2]))
    far_ws.append(swap(mlp_raws[2], "xh"))
    hid_one, hid_three = near(hidden, "z")

    attended = attend(queries, kv_parts)
    attended, hid_one, hid_three, far_ws[3] = lax.optimization_barrier((attended, hid_one, hid_three, far_ws[3]))
    out_ws = jnp.stack([jnp.concatenate([out_weight, mlp_out_weight]), jnp.concatenate(far_ws)])
    hid_low, hid_high = opposite(hid_one, hid_three, "z")
    attended = jnp.concatenate([attended[:rows], swap(attended[rows:], "xh")], axis=1)
    att_one, att_three = near(attended, "z")
    att_two = swap(attended, "z", 2)

    att_one, att_two, att_three, hid_low, hid_high, out_ws = lax.optimization_barrier(
        (att_one, att_two, att_three, hid_low, hid_high, out_ws)
    )
    att_parts = (attended, att_one, att_two, att_three)
    hid_keep, hid_give = (hidden, hid_one, hid_low, hid_three), (hidden, hid_one, hid_high, hid_three)

    got_sums = swap(project_out(att_parts, hid_give, 1, out_ws, xh, BF), "c")
    got_sums, raw_tokens, raw_targets = lax.optimization_barrier((got_sums, tokens, targets))

    base_rows = dyn(raw_tokens, mine * piece, piece, 0).reshape(piece, 8, block)
    goal_rows = dyn(raw_targets, mine * piece, piece, 0).reshape(piece, 8, target_block)
    spread_rows = jnp.concatenate([base_rows, goal_rows], axis=2).transpose(1, 0, 2)
    own_spread = lax.all_to_all(spread_rows, ("xh", "z"), split_axis=0, concat_axis=0, tiled=True)
    sums = project_out(att_parts, hid_keep, 0, out_ws, xh, BF)
    own, par = [sums[i].astype(F32) + got_sums[i].astype(F32) for i in range(2)]

    quarter = half // 4

    def chunks(x, start, count):
        return x[:, start * quarter : (start + count) * quarter]

    par_got = swap(chunks(par, 1, 2).astype(BF), "y", 1)
    own_got = swap(chunks(own, 2, 2).astype(BF), "y", 3)
    par_got, own_got, own_spread = lax.optimization_barrier((par_got, own_got, own_spread))
    base = own_spread[:, :, :block].reshape(8 * piece, block)
    own_goals = own_spread[:, :, block:].reshape(8 * piece, target_block)
    far_goals = swap(own_goals, "xl")
    par_next = swap((chunks(par, 3, 1) + chunks(par_got, 1, 1).astype(F32)).astype(BF), "y", 3)
    own_next = swap((chunks(own, 1, 1) + chunks(own_got, 0, 1).astype(F32)).astype(BF), "y", 1)
    par_next, own_next, far_goals = lax.optimization_barrier((par_next, own_next, far_goals))
    par_sum = chunks(par, 0, 1) + chunks(par_got, 0, 1).astype(F32) + par_next.astype(F32)
    own_sum = chunks(own, 0, 1) + chunks(own_got, 1, 1).astype(F32) + own_next.astype(F32)
    par_sum = par_sum.astype(BF)
    got_own = swap(own_sum[:, piece:].astype(BF), "xl")
    got_near = swap(par_sum[:, :piece], "xh")
    got_far = lax.ppermute(par_sum[:, piece:], ("xh", "xl"), [(i, i ^ 3) for i in range(4)])
    ours = own_sum[:, :piece] + got_own.astype(F32)
    theirs = got_near.astype(F32) + got_far.astype(F32)
    sum_own = in_order([ours[i] for i in range(4)], z)
    sum_theirs = in_order([theirs[i] for i in range(4)], z)
    total = both(xh, sum_own, sum_theirs)
    bias = dyn(out_bias, (xh * 4 + z) * block, block, 0)
    out_piece = (base.astype(F32) + bias + total).astype(BF)

    narrow = block // 2

    stay, leave = dyn(out_piece, c * narrow, narrow, 1), dyn(out_piece, (1 - c) * narrow, narrow, 1)
    pair = jnp.concatenate([stay, swap(leave, "c")])
    over_xl = swap(out_piece, "xl")
    pair = lax.ppermute(
        pair,
        ("xh", "z", "xl", "y"),
        [(a * 8 + b, b * 8 + a) for a in range(8) for b in range(8)],
    )
    pair, over_xl = lax.optimization_barrier((pair, over_xl))
    beside = jnp.concatenate([out_piece, own_goals], axis=1)
    over_xl_pair = jnp.concatenate([beside, jnp.concatenate([over_xl, far_goals], axis=1)])
    part_one, part_three = near(over_xl_pair, "y")
    pair = jnp.concatenate([pair, swap(pair, "xh")])
    col_one, col_three = near(pair, "z")
    low_rows, high_rows = part_one[: 8 * piece], part_three[8 * piece :]
    part_low, part_high = swap(low_rows, "y", 3), swap(high_rows, "y", 1)
    col_one, col_three, *_ = lax.optimization_barrier((col_one, col_three, low_rows, high_rows))
    col_low, col_high = opposite(col_one, col_three, "z")
    col_low, col_high, part_low, part_high = lax.optimization_barrier((col_low, col_high, part_low, part_high))
    columns = [pair, col_one, col_low, col_high, col_three]
    parts = [over_xl_pair, part_one, part_low, part_high, part_three]
    others = [swap(part, "c") for part in parts]
    return moments(columns, parts, others, jnp.stack([y ^ z, xh ^ xl]), block, rows * 8)


def solution(mesh):
    fine = Mesh(mesh.devices.reshape(2, 4, 2, 4, 2), ("xh", "z", "xl", "y", "c"))
    dp, mp = ("xh", "z"), ("xl", "y", "c")
    placed = (
        P(dp, None),
        P(),
        P(dp, None, mp),
        P(),
        P(dp, mp),
        P(mp),
        P(mp, dp),
        P(mp, dp),
        P(),
        P(dp, None),
    )
    return jax.shard_map(
        on_device,
        mesh=fine,
        in_specs=placed,
        out_specs=(P(mp, dp), P(mp, dp)),
        check_vma=False,
    )
```

```python
import functools

import jax
import jax.numpy as jnp
from jax import lax
from jax.experimental import pallas as pl
from jax.experimental.pallas import tpu as pltpu
from jax.sharding import Mesh, PartitionSpec as P

HEAD = 128
BF = jnp.bfloat16
F32 = jnp.float32
LOG2E = 1.4426950408889634


def layer_norm(inputs, norm_scale):
    center = jnp.mean(inputs, axis=-1, keepdims=True)
    spread = jnp.mean(jnp.square(inputs - center), axis=-1, keepdims=True)
    return (inputs - center) * lax.rsqrt(spread + 1e-06) * norm_scale


def swap(x, axis, mask=1):
    size = lax.axis_size(axis)
    return lax.ppermute(x, axis, [(i, i ^ mask) for i in range(size)])


def dyn(x, start, size, axis):
    return lax.dynamic_slice_in_dim(x, start, size, axis)


def dot(a, b):
    return jnp.dot(a, b, preferred_element_type=F32)


def after(x, *others):
    return lax.optimization_barrier((x,) + others)[0]


def near(x, axis):
    return swap(x, axis, 1), swap(x, axis, 3)


def opposite(one, three, axis):
    half = one.shape[0] // 2
    return swap(one[:half], axis, 3), swap(three[half:], axis, 1)


def ring_gather(x, axis):
    one, three = near(x, axis)
    return [x, one, jnp.concatenate(opposite(one, three, axis)), three]


def in_order(blocks, index):
    laid = [lax.select_n(index ^ i, *blocks) for i in range(len(blocks))]
    return jnp.concatenate(laid)


def both(flag, first, second, axis=0):
    return jnp.where(
        flag == 0,
        jnp.concatenate([first, second], axis=axis),
        jnp.concatenate([second, first], axis=axis),
    )


def norm_kernel(place, tokens_ref, gain_ref, *out_refs):
    block = tokens_ref.shape[1] // 8
    values = tokens_ref[...].astype(F32)
    center = jnp.mean(values, axis=-1, keepdims=True)
    spread = jnp.mean(jnp.square(values - center), axis=-1, keepdims=True)
    scale = lax.rsqrt(spread + 1e-06)
    for relative in range(4):
        column = pl.multiple_of((place[1] * 4 + (place[2] ^ relative)) * block, 128)
        part = tokens_ref[:, pl.ds(column, block)].astype(F32)
        normed = ((part - center) * scale * gain_ref[:, pl.ds(column, block)]).astype(BF)
        out_refs[relative][...] = normed


def norm_rows(tokens, gain, place, count, piece):
    width = tokens.shape[1]
    block = width // 8
    out = jax.ShapeDtypeStruct((count * piece, block), BF)
    return pl.pallas_call(
        norm_kernel,
        grid_spec=pltpu.PrefetchScalarGridSpec(
            num_scalar_prefetch=1,
            grid=(count,),
            in_specs=[
                pl.BlockSpec((piece, width), lambda i, place: (i ^ place[0], 0)),
                pl.BlockSpec((1, width), lambda i, place: (0, 0)),
            ],
            out_specs=[pl.BlockSpec((piece, block), lambda i, place: (i, 0))] * 4,
        ),
        out_shape=[out] * 4,
        compiler_params=pltpu.CompilerParams(vmem_limit_bytes=24 * 2**20),
        name="norm_rows",
    )(place, tokens, gain.reshape(1, width))


def attend_kernel(q_ref, *refs):
    kv_refs, out_ref = refs[:-1], refs[-1]
    queries = q_ref[...]
    scores = [
        lax.dot_general(queries, kv[:, :HEAD], (((1,), (1,)), ((), ())), preferred_element_type=F32)
        for kv in kv_refs
    ]
    top = functools.reduce(jnp.maximum, [jnp.max(s, axis=-1, keepdims=True) for s in scores])
    factor = HEAD ** (-0.5) * LOG2E
    total, mixed = 0.0, 0.0
    for part, kv in zip(scores, kv_refs):
        weights = jnp.exp2((part - top) * factor)
        total = total + jnp.sum(weights, axis=-1, keepdims=True)
        mixed = mixed + dot(weights.astype(BF), kv[:, HEAD:])
    out_ref[...] = (mixed / total).astype(BF)


def attend(queries, kv_parts):
    rows = queries.shape[0]
    step = min(256, rows)
    keys = sum(part.shape[0] for part in kv_parts)
    return pl.pallas_call(
        attend_kernel,
        grid=(rows // step,),
        in_specs=[pl.BlockSpec((step, HEAD), lambda i: (i, 0))]
        + [pl.BlockSpec(part.shape, lambda i: (0, 0), pipeline_mode=pl.Buffered(1)) for part in kv_parts],
        out_specs=pl.BlockSpec((step, HEAD), lambda i: (i, 0)),
        out_shape=jax.ShapeDtypeStruct((rows, HEAD), BF),
        compiler_params=pltpu.CompilerParams(vmem_limit_bytes=24 * 2**20),
        name="attend",
    )(queries, *kv_parts)


def pieces_dot(parts, weights, part=None):
    w0, w1, low, high, w3 = weights
    n0, n1, n2, n3 = parts
    half = n2.shape[1] // 2
    pairs = [(n0[...], w0), (n1[...], w1), (n3[...], w3), (n2[:, :half], low), (n2[:, half:], high)]
    total = None
    for rows, w in pairs:
        term = dot(rows, w[...] if part is None else w[part])
        total = term if total is None else total + term
    return total


def qkv_kernel(place, *refs):
    own, far, weights = refs[0:4], refs[4:8], refs[8:13]
    give_ref, keep_ref, hold = refs[13:]
    rows = own[0].shape[0]
    hold[:rows] = pieces_dot(own, weights, 0)
    hold[rows:] = pieces_dot(far, weights, 0)
    mine = pl.ds(pl.multiple_of(place[0] * HEAD, HEAD), HEAD)
    other = pl.ds(pl.multiple_of((1 - place[0]) * HEAD, HEAD), HEAD)
    keep_ref[...] = hold[:, mine]
    give_ref[:rows] = hold[rows:, other].astype(BF)
    give_ref[rows:] = hold[:rows, other].astype(BF)


def project_qkv(own, far, weights, xh):
    rows, block = own[0].shape

    def whole(x):
        return pl.BlockSpec(x.shape, lambda i, place: (0, 0), pipeline_mode=pl.Buffered(1))

    def third(w):
        return pl.BlockSpec((1,) + w.shape[1:], lambda i, place: (i, 0, 0))

    column = pl.BlockSpec((2 * rows, HEAD), lambda i, place: (0, i))
    return pl.pallas_call(
        qkv_kernel,
        grid_spec=pltpu.PrefetchScalarGridSpec(
            num_scalar_prefetch=1,
            grid=(3,),
            in_specs=[whole(x) for x in (*own, *far)] + [third(w) for w in weights],
            out_specs=[column, column],
            scratch_shapes=[pltpu.VMEM((2 * rows, 2 * HEAD), F32)],
        ),
        out_shape=[
            jax.ShapeDtypeStruct((2 * rows, 3 * HEAD), BF),
            jax.ShapeDtypeStruct((2 * rows, 3 * HEAD), F32),
        ],
        compiler_params=pltpu.CompilerParams(vmem_limit_bytes=32 * 2**20),
        name="project_qkv",
    )(jnp.reshape(xh, (1,)), *own, *far, *weights)


def mlp_kernel(*refs):
    refs[9][...] = pieces_dot(refs[0:4], refs[4:9]).astype(refs[9].dtype)


def project_mlp(parts, weights, dtype):
    rows, block = parts[0].shape
    wide = weights[0].shape[1]
    step = wide // 3
    return pl.pallas_call(
        mlp_kernel,
        grid=(3,),
        in_specs=[pl.BlockSpec(x.shape, lambda i: (0, 0), pipeline_mode=pl.Buffered(1)) for x in parts]
        + [pl.BlockSpec((w.shape[0], step), lambda i: (0, i)) for w in weights],
        out_specs=pl.BlockSpec((rows, step), lambda i: (0, i)),
        out_shape=jax.ShapeDtypeStruct((rows, wide), dtype),
        compiler_params=pltpu.CompilerParams(vmem_limit_bytes=48 * 2**20),
        name="project_mlp",
    )(*parts, *weights)


def output_kernel(place, *refs):
    attended, hidden, w_ref, out_ref = refs[0:4], refs[4:8], refs[8], refs[9]
    first = w_ref[0, pl.ds(pl.multiple_of(place[0] * HEAD, HEAD), HEAD)]
    second = w_ref[0, pl.ds(pl.multiple_of((1 - place[0]) * HEAD, HEAD), HEAD)]
    heads = jnp.concatenate([first, second])
    for i in range(4):
        a, h = attended[i], hidden[i]
        total = dot(h[...], w_ref[0, 2 * HEAD :]) + dot(a[...], heads)
        out_ref[0, i] = total.astype(out_ref.dtype)


def project_out(attended, hidden, which, weights, xh, dtype):
    rows = hidden[2].shape[0]
    _, depth, block = weights.shape

    def rows_of(x):
        at = 0 if x.shape[0] == rows else which
        return pl.BlockSpec((rows, x.shape[1]), lambda side, place: (at, 0), pipeline_mode=pl.Buffered(1))

    return pl.pallas_call(
        output_kernel,
        grid_spec=pltpu.PrefetchScalarGridSpec(
            num_scalar_prefetch=1,
            grid=(2,),
            in_specs=[rows_of(x) for x in (*attended, *hidden)]
            + [pl.BlockSpec((1, depth, block), lambda side, place: (side, 0, 0))],
            out_specs=pl.BlockSpec((1, 4, rows, block), lambda side, place: (side, 0, 0, 0)),
        ),
        out_shape=jax.ShapeDtypeStruct((2, 4, rows, block), dtype),
        compiler_params=pltpu.CompilerParams(vmem_limit_bytes=60 * 2**20),
        name="project_out",
    )(jnp.reshape(xh, (1,)), *attended, *hidden, weights)


def moment_kernel(total_tokens, place, *refs):
    columns, parts, others = refs[0:5], refs[5:10], refs[10:15]
    gram_ref, cross_ref, hold = refs[15:]
    tokens_here = hold.shape[3] // 2
    index = pl.program_id(0)

    @pl.when(index == 0)
    def _():
        for relative, ref in ((0, columns[0]), (1, columns[1]), (3, columns[4])):
            for side in range(2):
                rows = ref[side * 2 * tokens_here : (side + 1) * 2 * tokens_here]
                hold[relative ^ place[0], side ^ place[1]] = rows.T
        for side in range(2):
            hold[2 ^ place[0], side ^ place[1]] = columns[2 + side][...].T

    def part_rows(refs, relative, side):
        if relative == 2:
            return refs[2 + side][...]
        ref = refs[relative if relative < 2 else 4]
        return ref[side * tokens_here : (side + 1) * tokens_here]

    total = None
    for relative in range(4):
        for side in range(2):
            full = jnp.concatenate([part_rows(parts, relative, side), part_rows(others, relative, side)])
            term = dot(hold[relative, side], full)
            total = term if total is None else total + term
    total = total / total_tokens

    @pl.when(index < pl.num_programs(0) - 1)
    def _():
        gram_ref[...] = total

    @pl.when(index == pl.num_programs(0) - 1)
    def _():
        cross_ref[...] = total


def moments(columns, parts, others, place, block, total_tokens):
    narrow = columns[0].shape[1]
    step = parts[0].shape[1] - block
    steps = block // step
    kernel = functools.partial(moment_kernel, total_tokens)

    def whole(x):
        return pl.BlockSpec(x.shape, lambda i, place: (0, 0), pipeline_mode=pl.Buffered(1))

    def column(x):
        return pl.BlockSpec((x.shape[0], step), lambda i, place: (0, i))

    return pl.pallas_call(
        kernel,
        grid_spec=pltpu.PrefetchScalarGridSpec(
            num_scalar_prefetch=1,
            grid=(steps + 1,),
            in_specs=[whole(x) for x in columns] + [column(x) for x in (*parts, *others)],
            out_specs=[
                pl.BlockSpec((narrow, step), lambda i, place: (0, jnp.minimum(i, steps - 1))),
                pl.BlockSpec((narrow, step), lambda i, place: (0, 0)),
            ],
            scratch_shapes=[pltpu.VMEM((4, 2, narrow, columns[2].shape[0]), BF)],
        ),
        out_shape=[
            jax.ShapeDtypeStruct((narrow, block), F32),
            jax.ShapeDtypeStruct((narrow, step), F32),
        ],
        compiler_params=pltpu.CompilerParams(vmem_limit_bytes=60 * 2**20),
        name="moments",
    )(place, *columns, *parts, *others)


def on_device(
    tokens,
    norm_gain,
    qkv_weight,
    qk_gains,
    in_weight,
    in_bias,
    out_weight,
    mlp_out_weight,
    out_bias,
    targets,
):
    xh, z, xl, y, c = (lax.axis_index(a) for a in ("xh", "z", "xl", "y", "c"))
    rows, width = tokens.shape
    block = width // 8
    target_block = targets.shape[1] // 8
    piece = rows // 16
    half = rows // 2
    mine = (c * 4 + y) * 2 + xl

    qkv_w = qkv_weight.transpose(1, 0, 2)
    qkv_w1, qkv_w3 = near(qkv_w, "z")

    share = 2 * piece
    first_rows = dyn(tokens, (c * 4 + y) * share, share, 0)
    give_norm = norm_rows(first_rows, norm_gain, jnp.stack([xl, 1 - xh, z]), 2, piece)
    give_norm = jnp.concatenate(give_norm, axis=1)
    got = swap(give_norm, "xh")
    norm_own = norm_rows(after(tokens, give_norm), norm_gain, jnp.stack([mine, xh, z]), 16, piece)

    out_raw, got, *norm_own = lax.optimization_barrier((out_weight, got, *norm_own))
    depth = mlp_out_weight.shape[0] // 3
    mlp_raws = [mlp_out_weight[i * depth : (i + 1) * depth] for i in range(3)]
    far_ws = [swap(out_raw, "xh")]
    got_one, got_three = near(got, "y")
    got_one, got_three, qkv_w1, qkv_w3, far_ws[0], mlp_raws[0] = lax.optimization_barrier(
        (got_one, got_three, qkv_w1, qkv_w3, far_ws[0], mlp_raws[0])
    )
    far_ws.append(swap(mlp_raws[0], "xh"))
    middle = block // 2
    qkv_low = swap(qkv_w1[:, :middle], "z", 3)
    qkv_high = swap(qkv_w3[:, middle:], "z", 1)
    got_low, got_high = opposite(got_one, got_three, "y")
    got_low, got_high, qkv_low, qkv_high, in_raw, far_ws[1], mlp_raws[1] = lax.optimization_barrier(
        (got_low, got_high, qkv_low, qkv_high, in_weight, far_ws[1], mlp_raws[1])
    )
    far_ws.append(swap(mlp_raws[1], "xh"))
    around = jnp.concatenate([got, got_one, got_low, got_high, got_three])
    beyond = swap(around, "c")
    in_w1, in_w3 = near(in_raw, "z")
    norm_far = [
        jnp.concatenate([p[:, i * block : (i + 1) * block] for p in (around, beyond)]) for i in range(4)
    ]

    give, keep = project_qkv(norm_own, norm_far, (qkv_w, qkv_w1, qkv_low, qkv_high, qkv_w3), xh)
    give, far_ws[2] = lax.optimization_barrier((give, far_ws[2]))
    taken = swap(give, "xh")
    in_w1, in_w3, *norms = lax.optimization_barrier((in_w1, in_w3, *norm_own, *norm_far, give))
    norm_own, norm_far = norms[:4], norms[4:8]
    in_first, in_last = in_w1[:middle], in_w3[middle:]
    in_low, in_high = swap(in_first, "z", 3), swap(in_last, "z", 1)
    taken = after(taken, in_first, in_last)
    qkv = keep + taken.astype(F32)
    queries = layer_norm(qkv[:, :HEAD], qk_gains[0]).astype(BF)
    own_keys = layer_norm(qkv[:, HEAD : 2 * HEAD], qk_gains[1]).astype(BF)
    own_kv = jnp.concatenate([own_keys, qkv[:, 2 * HEAD :].astype(BF)], axis=1)
    kv_one, kv_three = near(own_kv, "z")

    in_ws = (in_weight, in_w1, in_low, in_high, in_w3)
    mlp_give = project_mlp(norm_far, in_ws, BF)
    mlp_far = swap(mlp_give, "xh")
    mlp_give, *norm_own = lax.optimization_barrier((mlp_give, *norm_own))
    mlp_own = project_mlp(norm_own, in_ws, F32)
    mlp_own, kv_one, kv_three = lax.optimization_barrier((mlp_own, kv_one, kv_three))
    kv_low, kv_high = opposite(kv_one, kv_three, "z")
    mlp_far, kv_low, kv_high = lax.optimization_barrier((mlp_far, kv_low, kv_high))
    kv_parts = [own_kv, kv_one, kv_three, kv_low, kv_high]
    mlp_input = mlp_own + mlp_far.astype(F32)
    hidden = jax.nn.gelu(mlp_input + in_bias, approximate=False).astype(BF)
    hidden, queries, mlp_raws[2] = lax.optimization_barrier((hidden, queries, mlp_raws[2]))
    far_ws.append(swap(mlp_raws[2], "xh"))
    hid_one, hid_three = near(hidden, "z")

    attended = attend(queries, kv_parts)
    attended, hid_one, hid_three, far_ws[3] = lax.optimization_barrier((attended, hid_one, hid_three, far_ws[3]))
    out_ws = jnp.stack([jnp.concatenate([out_weight, mlp_out_weight]), jnp.concatenate(far_ws)])
    hid_low, hid_high = opposite(hid_one, hid_three, "z")
    attended = jnp.concatenate([attended[:rows], swap(attended[rows:], "xh")], axis=1)
    att_one, att_three = near(attended, "z")
    att_two = swap(attended, "z", 2)

    att_one, att_two, att_three, hid_low, hid_high, out_ws = lax.optimization_barrier(
        (att_one, att_two, att_three, hid_low, hid_high, out_ws)
    )
    att_parts = (attended, att_one, att_two, att_three)
    hid_keep, hid_give = (hidden, hid_one, hid_low, hid_three), (hidden, hid_one, hid_high, hid_three)

    got_sums = swap(project_out(att_parts, hid_give, 1, out_ws, xh, BF), "c")
    got_sums, raw_tokens, raw_targets = lax.optimization_barrier((got_sums, tokens, targets))

    base_rows = dyn(raw_tokens, mine * piece, piece, 0).reshape(piece, 8, block)
    goal_rows = dyn(raw_targets, mine * piece, piece, 0).reshape(piece, 8, target_block)
    spread_rows = jnp.concatenate([base_rows, goal_rows], axis=2).transpose(1, 0, 2)
    own_spread = lax.all_to_all(spread_rows, ("xh", "z"), split_axis=0, concat_axis=0, tiled=True)
    sums = project_out(att_parts, hid_keep, 0, out_ws, xh, BF)
    own, par = [sums[i].astype(F32) + got_sums[i].astype(F32) for i in range(2)]

    quarter = half // 4

    def chunks(x, start, count):
        return x[:, start * quarter : (start + count) * quarter]

    par_got = swap(chunks(par, 1, 2).astype(BF), "y", 1)
    own_got = swap(chunks(own, 2, 2).astype(BF), "y", 3)
    par_got, own_got, own_spread = lax.optimization_barrier((par_got, own_got, own_spread))
    base = own_spread[:, :, :block].reshape(8 * piece, block)
    own_goals = own_spread[:, :, block:].reshape(8 * piece, target_block)
    far_goals = swap(own_goals, "xl")
    par_next = swap((chunks(par, 3, 1) + chunks(par_got, 1, 1).astype(F32)).astype(BF), "y", 3)
    own_next = swap((chunks(own, 1, 1) + chunks(own_got, 0, 1).astype(F32)).astype(BF), "y", 1)
    par_next, own_next, far_goals = lax.optimization_barrier((par_next, own_next, far_goals))
    par_sum = chunks(par, 0, 1) + chunks(par_got, 0, 1).astype(F32) + par_next.astype(F32)
    own_sum = chunks(own, 0, 1) + chunks(own_got, 1, 1).astype(F32) + own_next.astype(F32)
    par_sum = par_sum.astype(BF)
    got_own = swap(own_sum[:, piece:].astype(BF), "xl")
    got_near = swap(par_sum[:, :piece], "xh")
    got_far = lax.ppermute(par_sum[:, piece:], ("xh", "xl"), [(i, i ^ 3) for i in range(4)])
    ours = own_sum[:, :piece] + got_own.astype(F32)
    theirs = got_near.astype(F32) + got_far.astype(F32)
    sum_own = in_order([ours[i] for i in range(4)], z)
    sum_theirs = in_order([theirs[i] for i in range(4)], z)
    total = both(xh, sum_own, sum_theirs)
    bias = dyn(out_bias, (xh * 4 + z) * block, block, 0)
    out_piece = (base.astype(F32) + bias + total).astype(BF)

    narrow = block // 2

    stay, leave = dyn(out_piece, c * narrow, narrow, 1), dyn(out_piece, (1 - c) * narrow, narrow, 1)
    pair = jnp.concatenate([stay, swap(leave, "c")])
    over_xl = swap(out_piece, "xl")
    pair = lax.ppermute(
        pair,
        ("xh", "z", "xl", "y"),
        [(a * 8 + b, b * 8 + a) for a in range(8) for b in range(8)],
    )
    pair, over_xl = lax.optimization_barrier((pair, over_xl))
    beside = jnp.concatenate([out_piece, own_goals], axis=1)
    over_xl_pair = jnp.concatenate([beside, jnp.concatenate([over_xl, far_goals], axis=1)])
    part_one, part_three = near(over_xl_pair, "y")
    pair = jnp.concatenate([pair, swap(pair, "xh")])
    col_one, col_three = near(pair, "z")
    low_rows, high_rows = part_one[: 8 * piece], part_three[8 * piece :]
    part_low, part_high = swap(low_rows, "y", 3), swap(high_rows, "y", 1)
    col_one, col_three, *_ = lax.optimization_barrier((col_one, col_three, low_rows, high_rows))
    col_low, col_high = opposite(col_one, col_three, "z")
    col_low, col_high, part_low, part_high = lax.optimization_barrier((col_low, col_high, part_low, part_high))
    columns = [pair, col_one, col_low, col_high, col_three]
    parts = [over_xl_pair, part_one, part_low, part_high, part_three]
    others = [swap(part, "c") for part in parts]
    return moments(columns, parts, others, jnp.stack([y ^ z, xh ^ xl]), block, rows * 8)


def solution(mesh):
    fine = Mesh(mesh.devices.reshape(2, 4, 2, 4, 2), ("xh", "z", "xl", "y", "c"))
    dp, mp = ("xh", "z"), ("xl", "y", "c")
    placed = (
        P(dp, None),
        P(),
        P(dp, None, mp),
        P(),
        P(dp, mp),
        P(mp),
        P(mp, dp),
        P(mp, dp),
        P(),
        P(dp, None),
    )
    return jax.shard_map(
        on_device,
        mesh=fine,
        in_specs=placed,
        out_specs=(P(mp, dp), P(mp, dp)),
        check_vma=False,
    )
```

```python
import functools

import jax
import jax.numpy as jnp
from jax import lax
from jax.experimental import pallas as pl
from jax.experimental.pallas import tpu as pltpu
from jax.sharding import Mesh, PartitionSpec as P

HEAD = 128
BF = jnp.bfloat16
F32 = jnp.float32
LOG2E = 1.4426950408889634


def layer_norm(inputs, norm_scale):
    center = jnp.mean(inputs, axis=-1, keepdims=True)
    spread = jnp.mean(jnp.square(inputs - center), axis=-1, keepdims=True)
    return (inputs - center) * lax.rsqrt(spread + 1e-06) * norm_scale


def swap(x, axis, mask=1):
    size = lax.axis_size(axis)
    return lax.ppermute(x, axis, [(i, i ^ mask) for i in range(size)])


def dyn(x, start, size, axis):
    return lax.dynamic_slice_in_dim(x, start, size, axis)


def dot(a, b):
    return jnp.dot(a, b, preferred_element_type=F32)


def after(x, *others):
    return lax.optimization_barrier((x,) + others)[0]


def near(x, axis):
    return swap(x, axis, 1), swap(x, axis, 3)


def opposite(one, three, axis):
    half = one.shape[0] // 2
    return swap(one[:half], axis, 3), swap(three[half:], axis, 1)


def ring_gather(x, axis):
    one, three = near(x, axis)
    return [x, one, jnp.concatenate(opposite(one, three, axis)), three]


def in_order(blocks, index):
    laid = [lax.select_n(index ^ i, *blocks) for i in range(len(blocks))]
    return jnp.concatenate(laid)


def both(flag, first, second, axis=0):
    return jnp.where(
        flag == 0,
        jnp.concatenate([first, second], axis=axis),
        jnp.concatenate([second, first], axis=axis),
    )


def norm_kernel(place, tokens_ref, gain_ref, *out_refs):
    block = tokens_ref.shape[1] // 8
    values = tokens_ref[...].astype(F32)
    center = jnp.mean(values, axis=-1, keepdims=True)
    spread = jnp.mean(jnp.square(values - center), axis=-1, keepdims=True)
    scale = lax.rsqrt(spread + 1e-06)
    for relative in range(4):
        column = pl.multiple_of((place[1] * 4 + (place[2] ^ relative)) * block, 128)
        part = tokens_ref[:, pl.ds(column, block)].astype(F32)
        normed = ((part - center) * scale * gain_ref[:, pl.ds(column, block)]).astype(BF)
        out_refs[relative][...] = normed


def norm_rows(tokens, gain, place, count, piece):
    width = tokens.shape[1]
    block = width // 8
    out = jax.ShapeDtypeStruct((count * piece, block), BF)
    return pl.pallas_call(
        norm_kernel,
        grid_spec=pltpu.PrefetchScalarGridSpec(
            num_scalar_prefetch=1,
            grid=(count,),
            in_specs=[
                pl.BlockSpec((piece, width), lambda i, place: (i ^ place[0], 0)),
                pl.BlockSpec((1, width), lambda i, place: (0, 0)),
            ],
            out_specs=[pl.BlockSpec((piece, block), lambda i, place: (i, 0))] * 4,
        ),
        out_shape=[out] * 4,
        compiler_params=pltpu.CompilerParams(vmem_limit_bytes=24 * 2**20),
        name="norm_rows",
    )(place, tokens, gain.reshape(1, width))


def attend_kernel(q_ref, *refs):
    kv_refs, out_ref = refs[:-1], refs[-1]
    queries = q_ref[...]
    scores = [
        lax.dot_general(queries, kv[:, :HEAD], (((1,), (1,)), ((), ())), preferred_element_type=F32)
        for kv in kv_refs
    ]
    top = functools.reduce(jnp.maximum, [jnp.max(s, axis=-1, keepdims=True) for s in scores])
    factor = HEAD ** (-0.5) * LOG2E
    total, mixed = 0.0, 0.0
    for part, kv in zip(scores, kv_refs):
        weights = jnp.exp2((part - top) * factor)
        total = total + jnp.sum(weights, axis=-1, keepdims=True)
        mixed = mixed + dot(weights.astype(BF), kv[:, HEAD:])
    out_ref[...] = (mixed / total).astype(BF)


def attend(queries, kv_parts):
    rows = queries.shape[0]
    step = min(256, rows)
    keys = sum(part.shape[0] for part in kv_parts)
    return pl.pallas_call(
        attend_kernel,
        grid=(rows // step,),
        in_specs=[pl.BlockSpec((step, HEAD), lambda i: (i, 0))]
        + [pl.BlockSpec(part.shape, lambda i: (0, 0), pipeline_mode=pl.Buffered(1)) for part in kv_parts],
        out_specs=pl.BlockSpec((step, HEAD), lambda i: (i, 0)),
        out_shape=jax.ShapeDtypeStruct((rows, HEAD), BF),
        compiler_params=pltpu.CompilerParams(vmem_limit_bytes=24 * 2**20),
        name="attend",
    )(queries, *kv_parts)


def pieces_dot(parts, weights, part=None):
    w0, w1, low, high, w3 = weights
    n0, n1, n2, n3 = parts
    half = n2.shape[1] // 2
    pairs = [(n0[...], w0), (n1[...], w1), (n3[...], w3), (n2[:, :half], low), (n2[:, half:], high)]
    total = None
    for rows, w in pairs:
        term = dot(rows, w[...] if part is None else w[part])
        total = term if total is None else total + term
    return total


def qkv_kernel(place, *refs):
    own, far, weights = refs[0:4], refs[4:8], refs[8:13]
    give_ref, keep_ref, hold = refs[13:]
    rows = own[0].shape[0]
    hold[:rows] = pieces_dot(own, weights, 0)
    hold[rows:] = pieces_dot(far, weights, 0)
    mine = pl.ds(pl.multiple_of(place[0] * HEAD, HEAD), HEAD)
    other = pl.ds(pl.multiple_of((1 - place[0]) * HEAD, HEAD), HEAD)
    keep_ref[...] = hold[:, mine]
    give_ref[:rows] = hold[rows:, other].astype(BF)
    give_ref[rows:] = hold[:rows, other].astype(BF)


def project_qkv(own, far, weights, xh):
    rows, block = own[0].shape

    def whole(x):
        return pl.BlockSpec(x.shape, lambda i, place: (0, 0), pipeline_mode=pl.Buffered(1))

    def third(w):
        return pl.BlockSpec((1,) + w.shape[1:], lambda i, place: (i, 0, 0))

    column = pl.BlockSpec((2 * rows, HEAD), lambda i, place: (0, i))
    return pl.pallas_call(
        qkv_kernel,
        grid_spec=pltpu.PrefetchScalarGridSpec(
            num_scalar_prefetch=1,
            grid=(3,),
            in_specs=[whole(x) for x in (*own, *far)] + [third(w) for w in weights],
            out_specs=[column, column],
            scratch_shapes=[pltpu.VMEM((2 * rows, 2 * HEAD), F32)],
        ),
        out_shape=[
            jax.ShapeDtypeStruct((2 * rows, 3 * HEAD), BF),
            jax.ShapeDtypeStruct((2 * rows, 3 * HEAD), F32),
        ],
        compiler_params=pltpu.CompilerParams(vmem_limit_bytes=32 * 2**20),
        name="project_qkv",
    )(jnp.reshape(xh, (1,)), *own, *far, *weights)


def mlp_kernel(*refs):
    refs[9][...] = pieces_dot(refs[0:4], refs[4:9]).astype(refs[9].dtype)


def project_mlp(parts, weights, dtype):
    rows, block = parts[0].shape
    wide = weights[0].shape[1]
    step = wide // 3
    return pl.pallas_call(
        mlp_kernel,
        grid=(3,),
        in_specs=[pl.BlockSpec(x.shape, lambda i: (0, 0), pipeline_mode=pl.Buffered(1)) for x in parts]
        + [pl.BlockSpec((w.shape[0], step), lambda i: (0, i)) for w in weights],
        out_specs=pl.BlockSpec((rows, step), lambda i: (0, i)),
        out_shape=jax.ShapeDtypeStruct((rows, wide), dtype),
        compiler_params=pltpu.CompilerParams(vmem_limit_bytes=48 * 2**20),
        name="project_mlp",
    )(*parts, *weights)


def output_kernel(place, *refs):
    attended, hidden, w_ref, out_ref = refs[0:4], refs[4:8], refs[8], refs[9]
    first = w_ref[0, pl.ds(pl.multiple_of(place[0] * HEAD, HEAD), HEAD)]
    second = w_ref[0, pl.ds(pl.multiple_of((1 - place[0]) * HEAD, HEAD), HEAD)]
    heads = jnp.concatenate([first, second])
    for i in range(4):
        a, h = attended[i], hidden[i]
        total = dot(h[...], w_ref[0, 2 * HEAD :]) + dot(a[...], heads)
        out_ref[0, i] = total.astype(out_ref.dtype)


def project_out(attended, hidden, which, weights, xh, dtype):
    rows = hidden[2].shape[0]
    _, depth, block = weights.shape

    def rows_of(x):
        at = 0 if x.shape[0] == rows else which
        return pl.BlockSpec((rows, x.shape[1]), lambda side, place: (at, 0), pipeline_mode=pl.Buffered(1))

    return pl.pallas_call(
        output_kernel,
        grid_spec=pltpu.PrefetchScalarGridSpec(
            num_scalar_prefetch=1,
            grid=(2,),
            in_specs=[rows_of(x) for x in (*attended, *hidden)]
            + [pl.BlockSpec((1, depth, block), lambda side, place: (side, 0, 0))],
            out_specs=pl.BlockSpec((1, 4, rows, block), lambda side, place: (side, 0, 0, 0)),
        ),
        out_shape=jax.ShapeDtypeStruct((2, 4, rows, block), dtype),
        compiler_params=pltpu.CompilerParams(vmem_limit_bytes=60 * 2**20),
        name="project_out",
    )(jnp.reshape(xh, (1,)), *attended, *hidden, weights)


def moment_kernel(total_tokens, place, *refs):
    columns, parts, others = refs[0:5], refs[5:10], refs[10:15]
    gram_ref, cross_ref, hold = refs[15:]
    tokens_here = hold.shape[3] // 2
    index = pl.program_id(0)

    @pl.when(index == 0)
    def _():
        for relative, ref in ((0, columns[0]), (1, columns[1]), (3, columns[4])):
            for side in range(2):
                rows = ref[side * 2 * tokens_here : (side + 1) * 2 * tokens_here]
                hold[relative ^ place[0], side ^ place[1]] = rows.T
        for side in range(2):
            hold[2 ^ place[0], side ^ place[1]] = columns[2 + side][...].T

    def part_rows(refs, relative, side):
        if relative == 2:
            return refs[2 + side][...]
        ref = refs[relative if relative < 2 else 4]
        return ref[side * tokens_here : (side + 1) * tokens_here]

    total = None
    for relative in range(4):
        for side in range(2):
            full = jnp.concatenate([part_rows(parts, relative, side), part_rows(others, relative, side)])
            term = dot(hold[relative, side], full)
            total = term if total is None else total + term
    total = total / total_tokens

    @pl.when(index < pl.num_programs(0) - 1)
    def _():
        gram_ref[...] = total

    @pl.when(index == pl.num_programs(0) - 1)
    def _():
        cross_ref[...] = total


def moments(columns, parts, others, place, block, total_tokens):
    narrow = columns[0].shape[1]
    step = parts[0].shape[1] - block
    steps = block // step
    kernel = functools.partial(moment_kernel, total_tokens)

    def whole(x):
        return pl.BlockSpec(x.shape, lambda i, place: (0, 0), pipeline_mode=pl.Buffered(1))

    def column(x):
        return pl.BlockSpec((x.shape[0], step), lambda i, place: (0, i))

    return pl.pallas_call(
        kernel,
        grid_spec=pltpu.PrefetchScalarGridSpec(
            num_scalar_prefetch=1,
            grid=(steps + 1,),
            in_specs=[whole(x) for x in columns] + [column(x) for x in (*parts, *others)],
            out_specs=[
                pl.BlockSpec((narrow, step), lambda i, place: (0, jnp.minimum(i, steps - 1))),
                pl.BlockSpec((narrow, step), lambda i, place: (0, 0)),
            ],
            scratch_shapes=[pltpu.VMEM((4, 2, narrow, columns[2].shape[0]), BF)],
        ),
        out_shape=[
            jax.ShapeDtypeStruct((narrow, block), F32),
            jax.ShapeDtypeStruct((narrow, step), F32),
        ],
        compiler_params=pltpu.CompilerParams(vmem_limit_bytes=60 * 2**20),
        name="moments",
    )(place, *columns, *parts, *others)


def on_device(
    tokens,
    norm_gain,
    qkv_weight,
    qk_gains,
    in_weight,
    in_bias,
    out_weight,
    mlp_out_weight,
    out_bias,
    targets,
):
    xh, z, xl, y, c = (lax.axis_index(a) for a in ("xh", "z", "xl", "y", "c"))
    rows, width = tokens.shape
    block = width // 8
    target_block = targets.shape[1] // 8
    piece = rows // 16
    half = rows // 2
    mine = (c * 4 + y) * 2 + xl

    qkv_w = qkv_weight.transpose(1, 0, 2)
    qkv_w1, qkv_w3 = near(qkv_w, "z")

    share = 2 * piece
    first_rows = dyn(tokens, (c * 4 + y) * share, share, 0)
    give_norm = norm_rows(first_rows, norm_gain, jnp.stack([xl, 1 - xh, z]), 2, piece)
    give_norm = jnp.concatenate(give_norm, axis=1)
    got = swap(give_norm, "xh")
    norm_own = norm_rows(after(tokens, give_norm), norm_gain, jnp.stack([mine, xh, z]), 16, piece)

    out_raw, got, *norm_own = lax.optimization_barrier((out_weight, got, *norm_own))
    depth = mlp_out_weight.shape[0] // 3
    mlp_raws = [mlp_out_weight[i * depth : (i + 1) * depth] for i in range(3)]
    far_ws = [swap(out_raw, "xh")]
    got_one, got_three = near(got, "y")
    got_one, got_three, qkv_w1, qkv_w3, far_ws[0], mlp_raws[0] = lax.optimization_barrier(
        (got_one, got_three, qkv_w1, qkv_w3, far_ws[0], mlp_raws[0])
    )
    far_ws.append(swap(mlp_raws[0], "xh"))
    middle = block // 2
    qkv_low = swap(qkv_w1[:, :middle], "z", 3)
    qkv_high = swap(qkv_w3[:, middle:], "z", 1)
    got_low, got_high = opposite(got_one, got_three, "y")
    got_low, got_high, qkv_low, qkv_high, in_raw, far_ws[1], mlp_raws[1] = lax.optimization_barrier(
        (got_low, got_high, qkv_low, qkv_high, in_weight, far_ws[1], mlp_raws[1])
    )
    far_ws.append(swap(mlp_raws[1], "xh"))
    around = jnp.concatenate([got, got_one, got_low, got_high, got_three])
    beyond = swap(around, "c")
    in_w1, in_w3 = near(in_raw, "z")
    norm_far = [
        jnp.concatenate([p[:, i * block : (i + 1) * block] for p in (around, beyond)]) for i in range(4)
    ]

    give, keep = project_qkv(norm_own, norm_far, (qkv_w, qkv_w1, qkv_low, qkv_high, qkv_w3), xh)
    give, far_ws[2] = lax.optimization_barrier((give, far_ws[2]))
    taken = swap(give, "xh")
    in_w1, in_w3, *norms = lax.optimization_barrier((in_w1, in_w3, *norm_own, *norm_far, give))
    norm_own, norm_far = norms[:4], norms[4:8]
    in_first, in_last = in_w1[:middle], in_w3[middle:]
    in_low, in_high = swap(in_first, "z", 3), swap(in_last, "z", 1)
    taken = after(taken, in_first, in_last)
    qkv = keep + taken.astype(F32)
    queries = layer_norm(qkv[:, :HEAD], qk_gains[0]).astype(BF)
    own_keys = layer_norm(qkv[:, HEAD : 2 * HEAD], qk_gains[1]).astype(BF)
    own_kv = jnp.concatenate([own_keys, qkv[:, 2 * HEAD :].astype(BF)], axis=1)
    kv_one, kv_three = near(own_kv, "z")

    in_ws = (in_weight, in_w1, in_low, in_high, in_w3)
    early = dot(norm_far[0], in_weight) + dot(norm_far[1], in_w1) + dot(norm_far[3], in_w3)
    early, in_low, in_high = lax.optimization_barrier((early, in_low, in_high))
    in_ws = (in_weight, in_w1, in_low, in_high, in_w3)
    mlp_give = early + dot(norm_far[2][:, :middle], in_low) + dot(norm_far[2][:, middle:], in_high)
    mlp_give = mlp_give.astype(BF)
    mlp_far = swap(mlp_give, "xh")
    mlp_give, *norm_own = lax.optimization_barrier((mlp_give, *norm_own))
    mlp_own = project_mlp(norm_own, in_ws, F32)
    mlp_own, kv_one, kv_three = lax.optimization_barrier((mlp_own, kv_one, kv_three))
    kv_low, kv_high = opposite(kv_one, kv_three, "z")
    mlp_far, kv_low, kv_high = lax.optimization_barrier((mlp_far, kv_low, kv_high))
    kv_parts = [own_kv, kv_one, kv_three, kv_low, kv_high]
    mlp_input = mlp_own + mlp_far.astype(F32)
    hidden = jax.nn.gelu(mlp_input + in_bias, approximate=False).astype(BF)
    hidden, queries, mlp_raws[2] = lax.optimization_barrier((hidden, queries, mlp_raws[2]))
    far_ws.append(swap(mlp_raws[2], "xh"))
    hid_one, hid_three = near(hidden, "z")

    attended = attend(queries, kv_parts)
    attended, hid_one, hid_three, far_ws[3] = lax.optimization_barrier((attended, hid_one, hid_three, far_ws[3]))
    out_ws = jnp.stack([jnp.concatenate([out_weight, mlp_out_weight]), jnp.concatenate(far_ws)])
    hid_low, hid_high = opposite(hid_one, hid_three, "z")
    attended = jnp.concatenate([attended[:rows], swap(attended[rows:], "xh")], axis=1)
    att_one, att_three = near(attended, "z")
    att_two = swap(attended, "z", 2)

    att_one, att_two, att_three, hid_low, hid_high, out_ws = lax.optimization_barrier(
        (att_one, att_two, att_three, hid_low, hid_high, out_ws)
    )
    att_parts = (attended, att_one, att_two, att_three)
    hid_keep, hid_give = (hidden, hid_one, hid_low, hid_three), (hidden, hid_one, hid_high, hid_three)

    got_sums = swap(project_out(att_parts, hid_give, 1, out_ws, xh, BF), "c")
    got_sums, raw_tokens, raw_targets = lax.optimization_barrier((got_sums, tokens, targets))

    base_rows = dyn(raw_tokens, mine * piece, piece, 0).reshape(piece, 8, block)
    goal_rows = dyn(raw_targets, mine * piece, piece, 0).reshape(piece, 8, target_block)
    spread_rows = jnp.concatenate([base_rows, goal_rows], axis=2).transpose(1, 0, 2)
    own_spread = lax.all_to_all(spread_rows, ("xh", "z"), split_axis=0, concat_axis=0, tiled=True)
    sums = project_out(att_parts, hid_keep, 0, out_ws, xh, BF)
    own, par = [sums[i].astype(F32) + got_sums[i].astype(F32) for i in range(2)]

    quarter = half // 4

    def chunks(x, start, count):
        return x[:, start * quarter : (start + count) * quarter]

    par_got = swap(chunks(par, 1, 2).astype(BF), "y", 1)
    own_got = swap(chunks(own, 2, 2).astype(BF), "y", 3)
    par_got, own_got, own_spread = lax.optimization_barrier((par_got, own_got, own_spread))
    base = own_spread[:, :, :block].reshape(8 * piece, block)
    own_goals = own_spread[:, :, block:].reshape(8 * piece, target_block)
    far_goals = swap(own_goals, "xl")
    par_next = swap((chunks(par, 3, 1) + chunks(par_got, 1, 1).astype(F32)).astype(BF), "y", 3)
    own_next = swap((chunks(own, 1, 1) + chunks(own_got, 0, 1).astype(F32)).astype(BF), "y", 1)
    par_next, own_next, far_goals = lax.optimization_barrier((par_next, own_next, far_goals))
    par_sum = chunks(par, 0, 1) + chunks(par_got, 0, 1).astype(F32) + par_next.astype(F32)
    own_sum = chunks(own, 0, 1) + chunks(own_got, 1, 1).astype(F32) + own_next.astype(F32)
    par_sum = par_sum.astype(BF)
    got_own = swap(own_sum[:, piece:].astype(BF), "xl")
    got_near = swap(par_sum[:, :piece], "xh")
    got_far = lax.ppermute(par_sum[:, piece:], ("xh", "xl"), [(i, i ^ 3) for i in range(4)])
    ours = own_sum[:, :piece] + got_own.astype(F32)
    theirs = got_near.astype(F32) + got_far.astype(F32)
    sum_own = in_order([ours[i] for i in range(4)], z)
    sum_theirs = in_order([theirs[i] for i in range(4)], z)
    total = both(xh, sum_own, sum_theirs)
    bias = dyn(out_bias, (xh * 4 + z) * block, block, 0)
    out_piece = (base.astype(F32) + bias + total).astype(BF)

    narrow = block // 2

    stay, leave = dyn(out_piece, c * narrow, narrow, 1), dyn(out_piece, (1 - c) * narrow, narrow, 1)
    pair = jnp.concatenate([stay, swap(leave, "c")])
    over_xl = swap(out_piece, "xl")
    pair = lax.ppermute(
        pair,
        ("xh", "z", "xl", "y"),
        [(a * 8 + b, b * 8 + a) for a in range(8) for b in range(8)],
    )
    pair, over_xl = lax.optimization_barrier((pair, over_xl))
    beside = jnp.concatenate([out_piece, own_goals], axis=1)
    over_xl_pair = jnp.concatenate([beside, jnp.concatenate([over_xl, far_goals], axis=1)])
    part_one, part_three = near(over_xl_pair, "y")
    pair = jnp.concatenate([pair, swap(pair, "xh")])
    col_one, col_three = near(pair, "z")
    low_rows, high_rows = part_one[: 8 * piece], part_three[8 * piece :]
    part_low, part_high = swap(low_rows, "y", 3), swap(high_rows, "y", 1)
    col_one, col_three, *_ = lax.optimization_barrier((col_one, col_three, low_rows, high_rows))
    col_low, col_high = opposite(col_one, col_three, "z")
    col_low, col_high, part_low, part_high = lax.optimization_barrier((col_low, col_high, part_low, part_high))
    columns = [pair, col_one, col_low, col_high, col_three]
    parts = [over_xl_pair, part_one, part_low, part_high, part_three]
    others = [swap(part, "c") for part in parts]
    return moments(columns, parts, others, jnp.stack([y ^ z, xh ^ xl]), block, rows * 8)


def solution(mesh):
    fine = Mesh(mesh.devices.reshape(2, 4, 2, 4, 2), ("xh", "z", "xl", "y", "c"))
    dp, mp = ("xh", "z"), ("xl", "y", "c")
    placed = (
        P(dp, None),
        P(),
        P(dp, None, mp),
        P(),
        P(dp, mp),
        P(mp),
        P(mp, dp),
        P(mp, dp),
        P(),
        P(dp, None),
    )
    return jax.shard_map(
        on_device,
        mesh=fine,
        in_specs=placed,
        out_specs=(P(mp, dp), P(mp, dp)),
        check_vma=False,
    )
```
